128 devices in a mesh: section: 8 (over x_lo, z), dp: 16 (over y, x_hi, core).
Axes of the slice: x: 4 (x_hi: 2, x_lo: 2; x = x_hi * 2 + x_lo), y: 4, z: 4, core: 2. Of those that a mesh axis runs over, the one named last changes fastest.
Arguments:
- tokens: bfloat16 [5120, 3072], P('dp'), may hold values from -6 to 6
- cotangent: bfloat16 [5120, 3072], P('dp'), may hold values from -6 to 6
- live_counts: int32 [16, 4], P('dp'), may hold values from 1 to 80, 240 in all within a row
- weight: bfloat16 [8, 3072, 3072], P('section'), may hold values from -0.0546875 to 0.0546875
- inverse_in: float32 [8, 16, 192, 192], P('section', 'dp'), may hold values from -3 to 4, as said below
- inverse_out: float32 [8, 16, 192, 192], P('section'), may hold values from -3 to 4, as said below
Outputs:
- update: bfloat16 [8, 3072, 3072], P('section', 'dp')
- factor_in: float32 [8, 16, 192, 192], P('section', 'dp')
- factor_out: float32 [8, 16, 192, 192], P('section', 'dp')
The draws below stay inside these ranges and needn't reach their ends.
Inputs may be any that keep to these rules, and one draw needn't show every extreme that they name: `live_counts`: on each data rank the live counts of the micro-batches sum to 240, and one of them is 80. `inverse_in`: each block is symmetric. `inverse_out`: each block is symmetric.
All inputs are finite; a program needn't handle non-finite values.
Results may differ from the reference program's by a relative error of at most 0.025.
Values may be sent and summed in bfloat16 or wider, within the bound.
A program may use at most 192 MiB of HBM per device.

```python
import math
import jax
import jax.numpy as jnp
import numpy as np
from jax import lax

D = 3072
BLOCK = 192
MICRO = 4
ROWS = 80
TOK_DEV = 320
TOKENS = 5120
LAYERS = 8
NBLK = 16
N_DP = 16


def symmetric_blocks(key, diag_lo, diag_hi, spread):
    key_diag, key_off = jax.random.split(key)
    diag = jnp.exp(jax.random.uniform(key_diag, (LAYERS, NBLK, BLOCK), jnp.float32, jnp.log(diag_lo), jnp.log(diag_hi)))
    std = spread / (2.0 * BLOCK) ** 0.5
    noise = jnp.clip(jax.random.normal(key_off, (LAYERS, NBLK, BLOCK, BLOCK), jnp.float32), -4.0, 4.0) * std
    sym = noise + jnp.swapaxes(noise, 2, 3)
    eye = jnp.eye(BLOCK, dtype=jnp.float32)
    return sym * (1.0 - eye) + diag[:, :, :, None] * eye


def draw_inverse_in(key, part):
    key = jax.random.fold_in(key, 11)
    return symmetric_blocks(key, 0.5, 2.0, 0.5)


def draw_inverse_out(key, part):
    key = jax.random.fold_in(key, 23)
    return symmetric_blocks(key, 0.5, 2.0, 0.5)


def levels(key, shape, shards, low, high):
    gain = 1.0
    for dim, parts in shards:
        steps = jax.random.uniform(jax.random.fold_in(jax.random.fold_in(key, 6), dim), (parts,), jnp.float32, low / len(shards), high / len(shards))
        gain = gain * jnp.repeat(jnp.exp(steps), shape[dim] // parts).reshape((-1,) + (1,) * (len(shape) - 1 - dim))
    return gain


def split_up(number_of, total, most, lean):
    portions = [(1 << 20) // math.isqrt(grade ** lean) + 1 for grade in range(2, number_of + 1)]
    spare, given = total - most - (number_of - 1), [1] * (number_of - 1)
    while spare > 0:
        candidates = [i for i in range(number_of - 1) if given[i] < most]
        pool, remaining = sum([portions[i] for i in candidates]), spare
        for i in candidates:
            addition = min(most - given[i], max(1, remaining * portions[i] // pool), spare)
            given[i] = given[i] + addition
            spare = spare - addition
    return np.array([most] + given)


def uneven(rng, number_of, total, reach, skew):
    if number_of == 2:
        one = jax.random.randint(rng, (), max(1, total - reach), min(reach, total - 1) + 1)
        return jnp.stack([one, total - one])
    sizes = jnp.asarray(split_up(number_of, total, reach, skew), jnp.int32)
    twos = (number_of - 1) // 2
    source_of, sink = sizes[1:1 + 2 * twos:2], sizes[2:2 + 2 * twos:2]
    room = jnp.minimum(source_of - 1, reach - sink)
    moved = jax.random.randint(jax.random.fold_in(rng, 1), (twos,), 0, 1 << 20) % (room + 1)
    sizes = sizes.at[1:1 + 2 * twos:2].set(source_of - moved).at[2:2 + 2 * twos:2].set(sink + moved)
    return sizes[jax.random.permutation(jax.random.fold_in(rng, 2), number_of)]


def centred(own_key, shape, scale, reach, pieces=(), kind=jnp.bfloat16):
    array = scale * jax.random.normal(own_key, shape, jnp.float32)
    if pieces:
        array = array * levels(own_key, shape, pieces, -0.22, 0.18)
    return jnp.clip(array, -reach, reach).astype(kind)


def setup_inputs(seed: int = 0) -> dict:
    seeds = jax.random.split(jax.random.key(seed), 7)
    tokens = centred(seeds[0], (TOKENS, D), 1.0, 6.0, ((0, 16),))
    cotangent = centred(seeds[1], (TOKENS, D), 1.0, 6.0, ((0, 16),))
    live_counts = jax.vmap(lambda own: uneven(own, MICRO, 3 * ROWS, ROWS, 0))(jax.random.split(seeds[2], N_DP)).reshape((N_DP, MICRO)).astype(jnp.int32)
    weight = centred(seeds[3], (LAYERS, D, D), (4 * D) ** -0.5, 0.0546875, ((0, 8),))
    inverse_in = draw_inverse_in(jax.random.fold_in(seeds[6], 71), 0)
    inverse_out = draw_inverse_out(jax.random.fold_in(seeds[6], 71), 0)
    return dict(tokens=tokens, cotangent=cotangent, live_counts=live_counts, weight=weight, inverse_in=inverse_in, inverse_out=inverse_out)


C_ZERO = 0.7978845608028654
C_ONE = 0.044715

def activate(value):
    return 0.5 * value * (1.0 + jnp.tanh(C_ZERO * (value + C_ONE * value * value * value)))

def slope(value):
    hyper = jnp.tanh(C_ZERO * (value + C_ONE * value * value * value))
    return 0.5 * (1.0 + hyper) + 0.5 * value * (1.0 - hyper * hyper) * C_ZERO * (1.0 + 3.0 * C_ONE * value * value)

def block_gram(rows_data, total):
    blocks = rows_data.astype(jnp.float32).reshape(rows_data.shape[0], NBLK, BLOCK)
    return jnp.einsum('tkb,tkc->kbc', blocks, blocks) / total

def reference(tokens, cotangent, live_counts, weight, inverse_in, inverse_out):
    slots = jnp.arange(ROWS, dtype=jnp.int32)
    live = (slots[None, None, :] < live_counts[:, :, None]).reshape(TOKENS, 1).astype(jnp.float32)
    state = tokens
    inputs = []
    preacts = []
    for layer in range(LAYERS):
        pre = jnp.dot(state, weight[layer], preferred_element_type=jnp.float32)
        inputs.append(state)
        preacts.append(pre)
        state = (state.astype(jnp.float32) + activate(pre)).astype(jnp.bfloat16)
    flow = cotangent
    updates = [None] * LAYERS
    grams_in = [None] * LAYERS
    grams_out = [None] * LAYERS
    total = jnp.float32(TOKENS)
    for layer in range(LAYERS - 1, -1, -1):
        pre = preacts[layer]
        layer_in = inputs[layer]
        scaled = (flow.astype(jnp.float32) * slope(pre) * live).astype(jnp.bfloat16)
        flow = (flow.astype(jnp.float32) + jnp.dot(scaled, weight[layer].T, preferred_element_type=jnp.float32)).astype(jnp.bfloat16)

        def add_rank(carry, pair):
            rank_in, rank_scaled = pair
            term = jnp.dot(rank_in.T, rank_scaled, preferred_element_type=jnp.float32).astype(jnp.bfloat16)
            term = lax.optimization_barrier(term)
            return (carry + term.astype(jnp.float32), None)
        grad, unused = lax.scan(add_rank, jnp.zeros((D, D), jnp.float32), (layer_in.reshape(N_DP, TOK_DEV, D), scaled.reshape(N_DP, TOK_DEV, D)))
        live_in = layer_in * live.astype(jnp.bfloat16)
        grams_in[layer] = block_gram(live_in, total)
        grams_out[layer] = block_gram(scaled, total)
        left = jnp.einsum('kbc,kcd->kbd', inverse_in[layer], grad.reshape(NBLK, BLOCK, D), precision=lax.Precision.HIGHEST)
        right = jnp.einsum('rkc,kce->rke', left.reshape(D, NBLK, BLOCK), inverse_out[layer], precision=lax.Precision.HIGHEST)
        updates[layer] = (right.reshape(D, D) / jnp.sqrt(total)).astype(jnp.bfloat16)
    return (jnp.stack(updates), jnp.stack(grams_in), jnp.stack(grams_out))
```

```python
import functools

import jax
import jax.numpy as jnp
from jax import lax
from jax.experimental import pallas as pl
from jax.experimental.pallas import tpu as pltpu
from jax.sharding import PartitionSpec as P

D = 3072
HALF = D // 2
BLOCK = 192
MICRO = 4
ROWS = 80
TOK_DEV = 320
LIVE = 240
NBLK = 16
PAIR = 2 * LIVE
CHUNK = 48
CHUNKS = PAIR // CHUNK
PIECES = 3
WIDTH = HALF // PIECES

C_ZERO = 0.7978845608028654
C_ONE = 0.044715
MESH = pl.DeviceIdType.MESH


def activate(value):
    return 0.5 * value * (1.0 + jnp.tanh(C_ZERO * (value + C_ONE * value * value * value)))


def slope(value):
    hyper = jnp.tanh(C_ZERO * (value + C_ONE * value * value * value))
    return 0.5 * (1.0 + hyper) + 0.5 * value * (1.0 - hyper * hyper) * C_ZERO * (
        1.0 + 3.0 * C_ONE * value * value
    )


def block_gram(rows_data, total):
    blocks = rows_data.reshape(rows_data.shape[0], NBLK, BLOCK)
    return jnp.einsum("tkb,tkc->kbc", blocks, blocks, preferred_element_type=jnp.float32) / total


def mm(a, b):
    return jnp.dot(a, b, preferred_element_type=jnp.float32)


def pipeline(
    stages,
    source,
    weight,
    x_out,
    s_out,
    x_buf,
    s_buf,
    g_buf,
    slopes,
    f_send,
    b_send,
    w_fwd,
    w_bwd,
    w_raw,
    acc,
    load_sem,
    init_send,
    init_recv,
    f_send_sem,
    f_recv_sem,
    b_send_sem,
    b_recv_sem,
    xs_send_sem,
    xs_recv_sem,
    ss_send_sem,
    ss_recv_sem,
):
    stage = lax.axis_index("section")
    rank = lax.axis_index("dp")
    core = lax.rem(rank, 2)
    sibling = {"dp": rank + 1 - 2 * core}
    last = stages - 1
    following = {"section": jnp.minimum(stage + 1, last)}
    previous = {"section": jnp.maximum(stage - 1, 0)}
    own_cols = pl.ds(pl.multiple_of(core * HALF, HALF), HALF)
    sib_cols = pl.ds(pl.multiple_of((1 - core) * HALF, HALF), HALF)

    loads = (
        pltpu.make_async_copy(weight.at[own_cols, own_cols], w_fwd.at[0], load_sem.at[0]),
        pltpu.make_async_copy(weight.at[sib_cols, own_cols], w_fwd.at[1], load_sem.at[1]),
        pltpu.make_async_copy(weight.at[own_cols, sib_cols], w_raw, load_sem.at[2]),
    )
    for load in loads:
        load.start()

    barrier = pltpu.get_barrier_semaphore()
    pl.semaphore_signal(barrier, inc=1, device_id=sibling, device_id_type=MESH)

    @pl.when(stage > 0)
    def _():
        pl.semaphore_signal(barrier, inc=1, device_id=previous, device_id_type=MESH)

    @pl.when(stage < last)
    def _():
        pl.semaphore_signal(barrier, inc=1, device_id=following, device_id_type=MESH)

    pl.semaphore_wait(
        barrier, 1 + (stage > 0).astype(jnp.int32) + (stage < last).astype(jnp.int32)
    )

    mine = pl.ds(pl.multiple_of(core * LIVE, 16), LIVE)

    @pl.when(stage == 0)
    def _():
        moves = (
            pltpu.make_async_copy(source.at[core], x_buf.at[0, mine], load_sem.at[3]),
            pltpu.make_async_copy(source.at[1 - core], x_buf.at[1, mine], load_sem.at[4]),
            pltpu.make_async_remote_copy(
                source.at[1 - core], x_buf.at[0, mine], init_send.at[0], init_recv.at[0],
                device_id=sibling, device_id_type=MESH,
            ),
            pltpu.make_async_remote_copy(
                source.at[core], x_buf.at[1, mine], init_send.at[1], init_recv.at[1],
                device_id=sibling, device_id_type=MESH,
            ),
        )
        for move in moves:
            move.start()
        for move in moves:
            move.wait()

    @pl.when(stage == last)
    def _():
        moves = (
            pltpu.make_async_copy(source.at[core], g_buf.at[mine], load_sem.at[3]),
            pltpu.make_async_remote_copy(
                source.at[1 - core], g_buf.at[mine], init_send.at[0], init_recv.at[0],
                device_id=sibling, device_id_type=MESH,
            ),
        )
        for move in moves:
            move.start()
        for move in moves:
            move.wait()

    for load in loads:
        load.wait()

    def rows_of(k):
        return pl.ds(pl.multiple_of(k * CHUNK, 16), CHUNK)

    def cols_of(p):
        return pl.ds(p * WIDTH, WIDTH)

    def f_copy(k, p):
        return pltpu.make_async_remote_copy(
            f_send.at[rows_of(k), cols_of(p)], x_buf.at[0, rows_of(k), cols_of(p)],
            f_send_sem.at[k, p], f_recv_sem.at[k, p], device_id=following, device_id_type=MESH,
        )

    def b_copy(k, p):
        return pltpu.make_async_remote_copy(
            b_send.at[rows_of(k), cols_of(p)], g_buf.at[rows_of(k), cols_of(p)],
            b_send_sem.at[k, p], b_recv_sem.at[k, p], device_id=previous, device_id_type=MESH,
        )

    def x_copy(k, p):
        return pltpu.make_async_remote_copy(
            x_buf.at[0, rows_of(k), cols_of(p)], x_buf.at[1, rows_of(k), cols_of(p)],
            xs_send_sem.at[k, p], xs_recv_sem.at[k, p], device_id=sibling, device_id_type=MESH,
        )

    def s_copy(k, p):
        return pltpu.make_async_remote_copy(
            s_buf.at[0, rows_of(k), cols_of(p)], s_buf.at[1, rows_of(k), cols_of(p)],
            ss_send_sem.at[k, p], ss_recv_sem.at[k, p], device_id=sibling, device_id_type=MESH,
        )

    def forward(k):
        rows = rows_of(k)
        for p in range(PIECES):
            cols = cols_of(p)

            @pl.when(stage > 0)
            def _():
                f_copy(k, p).wait_recv()
                x_copy(k, p).start()

            term = mm(x_buf[0, rows, cols], w_fwd[0, cols, :])
            acc[...] = term if p == 0 else acc[...] + term
        for p in range(PIECES):

            @pl.when(stage > 0)
            def _():
                x_copy(k, p).wait_recv()

            cols = cols_of(p)
            if p < PIECES - 1:
                acc[...] += mm(x_buf[1, rows, cols], w_fwd[1, cols, :])
        end = cols_of(PIECES - 1)
        for p in range(PIECES):
            cols = cols_of(p)
            pre = acc[:, cols] + mm(x_buf[1, rows, end], w_fwd[1, end, cols])
            slopes[rows, cols] = pre

            @pl.when(stage < last)
            def _():
                f_send[rows, cols] = (
                    x_buf[0, rows, cols].astype(jnp.float32) + activate(pre)
                ).astype(jnp.bfloat16)
                f_copy(k, p).start()

        slopes[rows, :] = slope(slopes[rows, :])

    def backward(k):
        rows = rows_of(k)
        for p in range(PIECES):
            cols = cols_of(p)

            @pl.when(stage < last)
            def _():
                b_copy(k, p).wait_recv()

            s_buf[0, rows, cols] = (
                g_buf[rows, cols].astype(jnp.float32) * slopes[rows, cols]
            ).astype(jnp.bfloat16)
            s_copy(k, p).start()

            @pl.when(stage > 0)
            def _():
                term = mm(s_buf[0, rows, cols], w_bwd[0, cols, :])
                acc[...] = term if p == 0 else acc[...] + term

        for p in range(PIECES):
            s_copy(k, p).wait_recv()
            cols = cols_of(p)
            if p < PIECES - 1:

                @pl.when(stage > 0)
                def _():
                    acc[...] += mm(s_buf[1, rows, cols], w_bwd[1, cols, :])

        @pl.when(stage > 0)
        def _():
            end = cols_of(PIECES - 1)
            for p in range(PIECES):
                cols = cols_of(p)
                back = acc[:, cols] + mm(s_buf[1, rows, end], w_bwd[1, end, cols])
                b_send[rows, cols] = (
                    g_buf[rows, cols].astype(jnp.float32) + back
                ).astype(jnp.bfloat16)
                b_copy(k, p).start()

    turn_at = jnp.where(2 * stage + CHUNKS > 2 * last, 0, stage + CHUNKS)
    tile = 256

    def turn():
        def step(i, carry):
            at = pl.ds(pl.multiple_of(i * tile, tile), tile)
            for j in range(HALF // tile):
                to = pl.ds(j * tile, tile)
                w_bwd[0, to, at] = w_fwd[0, at, to].T
                w_bwd[1, to, at] = w_raw[at, to].T
            return carry

        lax.fori_loop(0, HALF // tile, step, 0)

    def slot(t, carry):
        @pl.when((t == turn_at) & (stage > 0))
        def _():
            turn()

        kf = t - stage

        @pl.when((kf >= 0) & (kf < CHUNKS))
        def _():
            forward(kf)

        kb = t - (2 * last - stage)

        @pl.when((kb >= 0) & (kb < CHUNKS))
        def _():
            backward(kb)

        return carry

    lax.fori_loop(0, 2 * last + CHUNKS, slot, 0)

    outs = (
        pltpu.make_async_copy(x_buf.at[0], x_out.at[core], load_sem.at[0]),
        pltpu.make_async_copy(x_buf.at[1], x_out.at[1 - core], load_sem.at[1]),
        pltpu.make_async_copy(s_buf.at[0], s_out.at[core], load_sem.at[2]),
        pltpu.make_async_copy(s_buf.at[1], s_out.at[1 - core], load_sem.at[3]),
    )
    for out in outs:
        out.start()

    def drain(k, carry):
        for p in range(PIECES):

            @pl.when(stage < last)
            def _():
                f_copy(k, p).wait_send()

            @pl.when(stage > 0)
            def _():
                x_copy(k, p).wait_send()
                b_copy(k, p).wait_send()

            s_copy(k, p).wait_send()
        return carry

    lax.fori_loop(0, CHUNKS, drain, 0)
    for out in outs:
        out.wait()


def run_pipeline(source, matrix):
    dma = pltpu.SemaphoreType.DMA
    any_space = pl.BlockSpec(memory_space=pl.ANY)
    pieces = (CHUNKS, PIECES)
    return pl.pallas_call(
        functools.partial(pipeline, lax.axis_size("section")),
        out_shape=[jax.ShapeDtypeStruct((2, PAIR, HALF), jnp.bfloat16)] * 2,
        in_specs=[any_space] * 2,
        out_specs=[any_space] * 2,
        scratch_shapes=[
            pltpu.VMEM((2, PAIR, HALF), jnp.bfloat16),
            pltpu.VMEM((2, PAIR, HALF), jnp.bfloat16),
            pltpu.VMEM((PAIR, HALF), jnp.bfloat16),
            pltpu.VMEM((PAIR, HALF), jnp.float32),
            pltpu.VMEM((PAIR, HALF), jnp.bfloat16),
            pltpu.VMEM((PAIR, HALF), jnp.bfloat16),
            pltpu.VMEM((2, HALF, HALF), jnp.bfloat16),
            pltpu.VMEM((2, HALF, HALF), jnp.bfloat16),
            pltpu.VMEM((HALF, HALF), jnp.bfloat16),
            pltpu.VMEM((CHUNK, HALF), jnp.float32),
            dma((5,)),
            dma((2,)),
            dma((2,)),
        ]
        + [dma(pieces)] * 8,
        compiler_params=pltpu.CompilerParams(
            collective_id=0, has_side_effects=True, vmem_limit_bytes=56 * 2**20
        ),
        name="pipeline",
    )(source, matrix)


def compact(counts, rows):
    ends = jnp.cumsum(counts)
    at = jnp.arange(LIVE, dtype=jnp.int32)
    micro = jnp.sum((at[:, None] >= ends[None, :]).astype(jnp.int32), axis=1)
    begin = ends - counts
    slot = micro * ROWS + at - jnp.sum(
        jnp.where(micro[:, None] == jnp.arange(MICRO)[None, :], begin[None, :], 0), axis=1
    )
    chosen = (slot[:, None] == jnp.arange(TOK_DEV, dtype=jnp.int32)[None, :]).astype(jnp.bfloat16)
    return jnp.stack(
        [
            mm(chosen, rows[:, :HALF]).astype(jnp.bfloat16),
            mm(chosen, rows[:, HALF:]).astype(jnp.bfloat16),
        ]
    )


def shards(tokens, cotangent, live_counts, weight, inverse_in, inverse_out):
    section_here = lax.axis_index("section")
    rank_count = lax.axis_size("dp")
    core = lax.rem(lax.axis_index("dp"), 2)
    total = jnp.float32(TOK_DEV * rank_count)
    source = compact(live_counts[0], jnp.where(section_here == 0, tokens, cotangent))
    x_pair, s_pair = run_pipeline(source, weight[0])

    def own(pair):
        part = lax.dynamic_slice_in_dim(pair, core * LIVE, LIVE, 1)
        return jnp.concatenate([part[0], part[1]], axis=1)

    in_flat = own(x_pair)
    scaled_flat = own(s_pair)
    gram_in = block_gram(in_flat, total)
    gram_out = block_gram(scaled_flat, total)
    owned_in, owned_out = (
        lax.psum_scatter(
            gram_in.astype(jnp.bfloat16), "dp", scatter_dimension=0, tiled=True
        ).astype(jnp.float32),
        lax.psum_scatter(
            gram_out.astype(jnp.bfloat16), "dp", scatter_dimension=0, tiled=True
        ).astype(jnp.float32),
    )
    owned_rows = D // rank_count
    grad_rows = lax.psum_scatter(
        lax.dot_general(
            in_flat, scaled_flat, (((0,), (0,)), ((), ())), preferred_element_type=jnp.float32
        ).astype(jnp.bfloat16),
        "dp",
        scatter_dimension=0,
        tiled=True,
    ).astype(jnp.float32)
    left = jnp.einsum(
        "kbc,kcd->kbd",
        inverse_in[0],
        grad_rows.reshape(owned_rows // BLOCK, BLOCK, D),
        precision=lax.Precision.HIGHEST,
    )
    right = jnp.einsum(
        "rkc,kce->rke",
        left.reshape(owned_rows, NBLK, BLOCK),
        inverse_out[0],
        precision=lax.Precision.HIGHEST,
    )
    update = (right.reshape(owned_rows, D) / jnp.sqrt(total)).astype(jnp.bfloat16)
    return (update[None], owned_in[None], owned_out[None])


def solution(mesh):
    in_specs = (
        P("dp", None),
        P("dp", None),
        P("dp", None),
        P("section", None, None),
        P("section", "dp", None, None),
        P("section", None, None, None),
    )
    out_specs = (
        P("section", "dp", None),
        P("section", "dp", None, None),
        P("section", "dp", None, None),
    )
    return jax.shard_map(shards, mesh=mesh, in_specs=in_specs, out_specs=out_specs, check_vma=False)
```

```python
import functools

import jax
import jax.numpy as jnp
from jax import lax
from jax.experimental import pallas as pl
from jax.experimental.pallas import tpu as pltpu
from jax.sharding import PartitionSpec as P

D = 3072
HALF = D // 2
BLOCK = 192
MICRO = 4
ROWS = 80
TOK_DEV = 320
LIVE = 240
NBLK = 16
PAIR = 2 * LIVE
CHUNK = 48
CHUNKS = PAIR // CHUNK
PIECES = 3
WIDTH = HALF // PIECES

C_ZERO = 0.7978845608028654
C_ONE = 0.044715
MESH = pl.DeviceIdType.MESH
RING = 4
QUAD = 4 * BLOCK
TWIN = 2 * BLOCK
TILES = HALF // TWIN
TOKENS = 5120


def activate(value):
    return 0.5 * value * (1.0 + jnp.tanh(C_ZERO * (value + C_ONE * value * value * value)))


def slope(value):
    hyper = jnp.tanh(C_ZERO * (value + C_ONE * value * value * value))
    return 0.5 * (1.0 + hyper) + 0.5 * value * (1.0 - hyper * hyper) * C_ZERO * (
        1.0 + 3.0 * C_ONE * value * value
    )


def mm(a, b):
    return jnp.dot(a, b, preferred_element_type=jnp.float32)


def gram(a, b):
    return lax.dot_general(a, b, (((0,), (0,)), ((), ())), preferred_element_type=jnp.float32)


def pipeline(
    stages,
    source,
    weight,
    inv_in,
    inv_out,
    update,
    gram_in,
    gram_out,
    x_buf,
    s_all,
    s_sib,
    g_buf,
    slopes,
    f_send,
    b_send,
    w_fwd,
    w_bwd,
    w_raw,
    acc,
    x_all,
    x_turned,
    d_send,
    d_recv,
    d_own,
    r_send,
    r_recv,
    p_raw,
    p_in,
    p_out,
    square,
    gi_send,
    gi_recv,
    go_send,
    go_recv,
    load_sem,
    init_send,
    init_recv,
    f_send_sem,
    f_recv_sem,
    b_send_sem,
    b_recv_sem,
    xs_send_sem,
    xs_recv_sem,
    ss_send_sem,
    ss_recv_sem,
    xa_send_sem,
    xa_recv_sem,
    sa_send_sem,
    sa_recv_sem,
    d_send_sem,
    d_recv_sem,
    r_send_sem,
    r_recv_sem,
    gi_sem,
    go_send_sem,
    go_recv_sem,
):
    stage = lax.axis_index("section")
    rank = lax.axis_index("dp")
    core = lax.rem(rank, 2)
    side = lax.rem(rank // 2, 2)
    ring = rank // 4
    sibling = {"dp": rank + 1 - 2 * core}
    across = {"dp": rank + 2 - 4 * side}
    last = stages - 1
    following = {"section": jnp.minimum(stage + 1, last)}
    previous = {"section": jnp.maximum(stage - 1, 0)}
    own_cols = pl.ds(pl.multiple_of(core * HALF, HALF), HALF)
    sib_cols = pl.ds(pl.multiple_of((1 - core) * HALF, HALF), HALF)

    def ring_at(d):
        return lax.rem(ring + d, RING)

    def ring_peer(d):
        return {"dp": ring_at(d) * 4 + lax.rem(rank, 4)}

    def go_rank(e):
        return (2 * core + ring // 2) * 4 + lax.rem(ring, 2) * 2 + e

    def go_source(h):
        return (2 * lax.rem(ring, 2) + side) * 4 + h * 2 + ring // 2

    loads = (
        pltpu.make_async_copy(weight.at[own_cols, own_cols], w_fwd.at[0], load_sem.at[0]),
        pltpu.make_async_copy(weight.at[sib_cols, own_cols], w_fwd.at[1], load_sem.at[1]),
        pltpu.make_async_copy(weight.at[own_cols, sib_cols], w_raw, load_sem.at[2]),
    )
    for load in loads:
        load.start()

    barrier = pltpu.get_barrier_semaphore()

    def greet(device):
        pl.semaphore_signal(barrier, inc=1, device_id=device, device_id_type=MESH)

    greet(sibling)
    greet(across)
    for d in range(1, RING):
        greet(ring_peer(d))

    @pl.when(stage > 0)
    def _():
        greet(previous)

    @pl.when(stage < last)
    def _():
        greet(following)

    for h in range(2):

        @pl.when(go_source(h) != rank)
        def _():
            greet({"dp": go_source(h)})

    expected = 5 + (stage > 0).astype(jnp.int32) + (stage < last).astype(jnp.int32)
    for e in range(2):
        expected = expected + (go_rank(e) != rank).astype(jnp.int32)
    pl.semaphore_wait(barrier, expected)

    mine = pl.ds(pl.multiple_of(core * LIVE, 16), LIVE)

    @pl.when(stage == 0)
    def _():
        moves = (
            pltpu.make_async_copy(source.at[core], x_buf.at[0, mine], load_sem.at[3]),
            pltpu.make_async_copy(source.at[1 - core], x_buf.at[1, mine], load_sem.at[4]),
            pltpu.make_async_remote_copy(
                source.at[1 - core], x_buf.at[0, mine], init_send.at[0], init_recv.at[0],
                device_id=sibling, device_id_type=MESH,
            ),
            pltpu.make_async_remote_copy(
                source.at[core], x_buf.at[1, mine], init_send.at[1], init_recv.at[1],
                device_id=sibling, device_id_type=MESH,
            ),
        )
        for move in moves:
            move.start()
        for move in moves:
            move.wait()

    @pl.when(stage == last)
    def _():
        moves = (
            pltpu.make_async_copy(source.at[core], g_buf.at[mine], load_sem.at[3]),
            pltpu.make_async_remote_copy(
                source.at[1 - core], g_buf.at[mine], init_send.at[0], init_recv.at[0],
                device_id=sibling, device_id_type=MESH,
            ),
        )
        for move in moves:
            move.start()
        for move in moves:
            move.wait()

    for load in loads:
        load.wait()

    def rows_of(k):
        return pl.ds(pl.multiple_of(k * CHUNK, 16), CHUNK)

    def cols_of(p):
        return pl.ds(p * WIDTH, WIDTH)

    def remote(src, dst, send, recv, device):
        return pltpu.make_async_remote_copy(
            src, dst, send, recv, device_id=device, device_id_type=MESH
        )

    def f_copy(k, p):
        at = (rows_of(k), cols_of(p))
        return remote(
            f_send.at[at], x_buf.at[(0,) + at], f_send_sem.at[k, p], f_recv_sem.at[k, p], following
        )

    def b_copy(k, p):
        at = (rows_of(k), cols_of(p))
        return remote(
            b_send.at[at], g_buf.at[at], b_send_sem.at[k, p], b_recv_sem.at[k, p], previous
        )

    def x_copy(k, p):
        at = (rows_of(k), cols_of(p))
        return remote(
            x_buf.at[(0,) + at], x_buf.at[(1,) + at], xs_send_sem.at[k, p], xs_recv_sem.at[k, p],
            sibling,
        )

    def s_copy(k, p):
        at = (rows_of(k), cols_of(p))
        return remote(
            s_all.at[(ring,) + at], s_sib.at[at], ss_send_sem.at[k, p], ss_recv_sem.at[k, p], sibling
        )

    def quad_of(r):
        which = jnp.where(r // 2 == core, 0, 1)
        return which, pl.ds(pl.multiple_of(lax.rem(r, 2) * QUAD, QUAD), QUAD)

    def xa_send(k, d):
        which, cols = quad_of(ring_at(d))
        return remote(
            x_buf.at[which, rows_of(k), cols], x_all.at[ring, rows_of(k)],
            xa_send_sem.at[k, d - 1], xa_recv_sem.at[k, d - 1], ring_peer(d),
        )

    def xa_recv(k, d):
        here = x_all.at[ring_at(RING - d), rows_of(k)]
        return remote(here, here, xa_send_sem.at[k, d - 1], xa_recv_sem.at[k, d - 1], ring_peer(d))

    def sa_send(k, d):
        here = s_all.at[ring, rows_of(k)]
        return remote(here, here, sa_send_sem.at[k, d - 1], sa_recv_sem.at[k, d - 1], ring_peer(d))

    def sa_recv(k, d):
        here = s_all.at[ring_at(RING - d), rows_of(k)]
        return remote(here, here, sa_send_sem.at[k, d - 1], sa_recv_sem.at[k, d - 1], ring_peer(d))

    def forward(k):
        rows = rows_of(k)
        for p in range(PIECES):
            cols = cols_of(p)

            @pl.when(stage > 0)
            def _():
                f_copy(k, p).wait_recv()
                x_copy(k, p).start()

            term = mm(x_buf[0, rows, cols], w_fwd[0, cols, :])
            acc[...] = term if p == 0 else acc[...] + term
        for p in range(PIECES):

            @pl.when(stage > 0)
            def _():
                x_copy(k, p).wait_recv()

            cols = cols_of(p)
            if p < PIECES - 1:
                acc[...] += mm(x_buf[1, rows, cols], w_fwd[1, cols, :])
        end = cols_of(PIECES - 1)
        for p in range(PIECES):
            cols = cols_of(p)
            pre = acc[:, cols] + mm(x_buf[1, rows, end], w_fwd[1, end, cols])
            slopes[rows, cols] = pre

            @pl.when(stage < last)
            def _():
                f_send[rows, cols] = (
                    x_buf[0, rows, cols].astype(jnp.float32) + activate(pre)
                ).astype(jnp.bfloat16)
                f_copy(k, p).start()

        for d in range(1, RING):
            xa_send(k, d).start()
        slopes[rows, :] = slope(slopes[rows, :])
        which, cols = quad_of(ring)
        x_all[ring, rows, :] = x_buf[which, rows, cols]

    def backward(k):
        rows = rows_of(k)
        for p in range(PIECES):
            cols = cols_of(p)

            @pl.when(stage < last)
            def _():
                b_copy(k, p).wait_recv()

            s_all[ring, rows, cols] = (
                g_buf[rows, cols].astype(jnp.float32) * slopes[rows, cols]
            ).astype(jnp.bfloat16)
            s_copy(k, p).start()

            @pl.when(stage > 0)
            def _():
                term = mm(s_all[ring, rows, cols], w_bwd[0, cols, :])
                acc[...] = term if p == 0 else acc[...] + term

        @pl.when(stage == 0)
        def _():
            for d in range(1, RING):
                sa_send(k, d).start()

        for p in range(PIECES):
            s_copy(k, p).wait_recv()
            cols = cols_of(p)
            if p < PIECES - 1:

                @pl.when(stage > 0)
                def _():
                    acc[...] += mm(s_sib[rows, cols], w_bwd[1, cols, :])

        @pl.when(stage > 0)
        def _():
            end = cols_of(PIECES - 1)
            for p in range(PIECES):
                cols = cols_of(p)
                back = acc[:, cols] + mm(s_sib[rows, end], w_bwd[1, end, cols])
                b_send[rows, cols] = (
                    g_buf[rows, cols].astype(jnp.float32) + back
                ).astype(jnp.bfloat16)
                b_copy(k, p).start()
            for d in range(1, RING):
                sa_send(k, d).start()

    turn_at = jnp.where(2 * stage + CHUNKS > 2 * last, 0, stage + CHUNKS)
    tile = 256

    def turn():
        @pl.when(stage > 0)
        def _():
            def step(i, carry):
                at = pl.ds(pl.multiple_of(i * tile, tile), tile)
                for j in range(HALF // tile):
                    to = pl.ds(j * tile, tile)
                    w_bwd[0, to, at] = w_fwd[0, at, to].T
                    w_bwd[1, to, at] = w_raw[at, to].T
                return carry

            lax.fori_loop(0, HALF // tile, step, 0)

        load = pltpu.make_async_copy(inv_in, p_raw.at[0], load_sem.at[0])
        load.start()
        load.wait()
        p_in[...] = p_raw[0].astype(jnp.bfloat16)
        p_out[...] = jnp.zeros_like(p_out)

        def step(i, carry):
            pair = pltpu.make_async_copy(inv_out.at[pl.ds(2 * i, 2)], p_raw, load_sem.at[0])
            pair.start()
            pair.wait()
            p_out[i, 0:BLOCK, 0:BLOCK] = p_raw[0].astype(jnp.bfloat16)
            p_out[i, BLOCK:TWIN, BLOCK:TWIN] = p_raw[1].astype(jnp.bfloat16)
            return carry

        lax.fori_loop(0, 2 * TILES, step, 0)

    def twin_of(h):
        return pl.ds(pl.multiple_of(h * TWIN, TWIN), TWIN)

    gi_copy = remote(gi_send, gi_recv, gi_sem.at[0], gi_sem.at[1], across)

    def collect_x():
        def arrive(k, carry):
            for d in range(1, RING):
                xa_recv(k, d).wait_recv()
            return carry

        lax.fori_loop(0, CHUNKS, arrive, 0)

        def turn_x(r, carry):
            for j in range(QUAD // tile):
                cols = pl.ds(j * tile, tile)
                x_turned[r, cols, :] = x_all[r, :, cols].T
            return carry

        lax.fori_loop(0, RING, turn_x, 0)
        for part in range(2):
            half = 1 - side if part == 0 else side
            rows = pl.ds(pl.multiple_of(half * TWIN + core * BLOCK, 16), BLOCK)
            both = jnp.zeros((BLOCK, TWIN), jnp.float32)
            for r in range(RING):
                both += mm(x_turned[r, rows, :], x_all[r, :, twin_of(half)])
            square[0:BLOCK, :] = both * (1.0 / TOKENS)
            target = gi_send if part == 0 else gram_in
            for e in range(2):

                @pl.when(core == e)
                def _():
                    target[...] = square[0:BLOCK, e * BLOCK : (e + 1) * BLOCK]

            if part == 0:
                gi_copy.start()

    collect_at = stage + CHUNKS + 6

    def slot(t, carry):
        @pl.when(t == turn_at)
        def _():
            turn()

        kf = t - stage

        @pl.when((kf >= 0) & (kf < CHUNKS))
        def _():
            forward(kf)

        kb = t - (2 * last - stage)

        @pl.when((kb >= 0) & (kb < CHUNKS))
        def _():
            backward(kb)

        @pl.when(t == collect_at)
        def _():
            collect_x()

        return carry

    lax.fori_loop(0, 2 * last + CHUNKS, slot, 0)

    def arrive(k, carry):
        for d in range(1, RING):
            sa_recv(k, d).wait_recv()
        return carry

    lax.fori_loop(0, CHUNKS, arrive, 0)

    def partial(half, j):
        cols = pl.ds(pl.multiple_of(j * TWIN, TWIN), TWIN)
        total = mm(x_turned[0, twin_of(half), :], s_all[0, :, cols])
        for r in range(1, RING):
            total += mm(x_turned[r, twin_of(half), :], s_all[r, :, cols])
        return total

    def d_copy(j):
        return remote(d_send.at[j], d_recv.at[j], d_send_sem.at[j], d_recv_sem.at[j], across)

    def r_copy(j):
        return remote(r_send.at[j], r_recv.at[j], r_send_sem.at[j], r_recv_sem.at[j], sibling)

    def theirs(j, carry):
        d_send[j] = partial(1 - side, j).astype(jnp.bfloat16)
        d_copy(j).start()
        return carry

    lax.fori_loop(0, TILES, theirs, 0)

    square[...] = jnp.zeros_like(square)
    for r in range(RING):
        cols = twin_of(ring)
        square[...] += gram(s_all[r, :, cols], s_all[r, :, cols])

    def go_remote(e, device):
        return remote(go_send.at[e], go_recv.at[side], go_send_sem.at[e], go_recv_sem.at[side], device)

    def go_local(e):
        return pltpu.make_async_copy(go_send.at[e], go_recv.at[side], go_recv_sem.at[side])

    for e in range(2):
        span = slice(e * BLOCK, (e + 1) * BLOCK)
        go_send[e] = square[span, span] * (1.0 / TOKENS)

        @pl.when(go_rank(e) == rank)
        def _():
            go_local(e).start()

        @pl.when(go_rank(e) != rank)
        def _():
            go_remote(e, {"dp": go_rank(e)}).start()

    def ours(j, carry):
        d_own[j] = partial(side, j)
        return carry

    lax.fori_loop(0, TILES, ours, 0)

    def condition(grad, which, j):
        left = mm(p_in[...], grad).astype(jnp.bfloat16)
        right = mm(left, p_out[which * TILES + j]) * (1.0 / TOKENS**0.5)
        at = pl.ds(pl.multiple_of(which * HALF + j * TWIN, TWIN), TWIN)
        update[:, at] = right.astype(jnp.bfloat16)

    def settle(j, carry):
        d_copy(j).wait_recv()
        d_own[j] = d_own[j] + d_recv[j].astype(jnp.float32)
        theirs_at = pl.ds(pl.multiple_of((1 - core) * BLOCK, 16), BLOCK)
        ours_at = pl.ds(pl.multiple_of(core * BLOCK, 16), BLOCK)
        r_send[j] = d_own[j, theirs_at, :].astype(jnp.bfloat16)
        r_copy(j).start()
        condition(d_own[j, ours_at, :].astype(jnp.bfloat16), core, j)
        return carry

    lax.fori_loop(0, TILES, settle, 0)

    def finish(j, carry):
        r_copy(j).wait_recv()
        condition(r_recv[j], 1 - core, j)
        return carry

    lax.fori_loop(0, TILES, finish, 0)

    gi_copy.wait()
    gram_in[...] += gi_recv[...]
    for h in range(2):
        own = go_source(h) == rank

        @pl.when(own)
        def _():
            pltpu.make_async_copy(go_send.at[0], go_recv.at[h], go_recv_sem.at[h]).wait()

        @pl.when(jnp.logical_not(own))
        def _():
            remote(
                go_send.at[0], go_recv.at[h], go_send_sem.at[0], go_recv_sem.at[h], sibling
            ).wait_recv()

    gram_out[...] = go_recv[0] + go_recv[1]

    def drain(k, carry):
        for p in range(PIECES):

            @pl.when(stage < last)
            def _():
                f_copy(k, p).wait_send()

            @pl.when(stage > 0)
            def _():
                x_copy(k, p).wait_send()
                b_copy(k, p).wait_send()

            s_copy(k, p).wait_send()
        for d in range(1, RING):
            xa_send(k, d).wait_send()
            sa_send(k, d).wait_send()
        return carry

    lax.fori_loop(0, CHUNKS, drain, 0)
    for j in range(TILES):
        d_copy(j).wait_send()
        r_copy(j).wait_send()
    for e in range(2):

        @pl.when(go_rank(e) != rank)
        def _():
            go_remote(e, sibling).wait_send()


def run_pipeline(source, matrix, inverse_in, inverse_out):
    dma = pltpu.SemaphoreType.DMA
    any_space = pl.BlockSpec(memory_space=pl.ANY)
    in_vmem = pl.BlockSpec(memory_space=pltpu.VMEM)
    pieces = (CHUNKS, PIECES)
    peers = (CHUNKS, RING - 1)
    bf16, f32 = jnp.bfloat16, jnp.float32
    return pl.pallas_call(
        functools.partial(pipeline, lax.axis_size("section")),
        out_shape=[
            jax.ShapeDtypeStruct((BLOCK, D), bf16),
            jax.ShapeDtypeStruct((BLOCK, BLOCK), f32),
            jax.ShapeDtypeStruct((BLOCK, BLOCK), f32),
        ],
        in_specs=[any_space] * 4,
        out_specs=[in_vmem] * 3,
        scratch_shapes=[
            pltpu.VMEM((2, PAIR, HALF), bf16),
            pltpu.VMEM((RING, PAIR, HALF), bf16),
            pltpu.VMEM((PAIR, HALF), bf16),
            pltpu.VMEM((PAIR, HALF), bf16),
            pltpu.VMEM((PAIR, HALF), f32),
            pltpu.VMEM((PAIR, HALF), bf16),
            pltpu.VMEM((PAIR, HALF), bf16),
            pltpu.VMEM((2, HALF, HALF), bf16),
            pltpu.VMEM((2, HALF, HALF), bf16),
            pltpu.VMEM((HALF, HALF), bf16),
            pltpu.VMEM((CHUNK, HALF), f32),
            pltpu.VMEM((RING, PAIR, QUAD), bf16),
            pltpu.VMEM((RING, QUAD, PAIR), bf16),
            pltpu.VMEM((TILES, TWIN, TWIN), bf16),
            pltpu.VMEM((TILES, TWIN, TWIN), bf16),
            pltpu.VMEM((TILES, TWIN, TWIN), f32),
            pltpu.VMEM((TILES, BLOCK, TWIN), bf16),
            pltpu.VMEM((TILES, BLOCK, TWIN), bf16),
            pltpu.VMEM((2, BLOCK, BLOCK), f32),
            pltpu.VMEM((BLOCK, BLOCK), bf16),
            pltpu.VMEM((2 * TILES, TWIN, TWIN), bf16),
            pltpu.VMEM((TWIN, TWIN), f32),
            pltpu.VMEM((BLOCK, BLOCK), f32),
            pltpu.VMEM((BLOCK, BLOCK), f32),
            pltpu.VMEM((2, BLOCK, BLOCK), f32),
            pltpu.VMEM((2, BLOCK, BLOCK), f32),
            dma((5,)),
            dma((2,)),
            dma((2,)),
        ]
        + [dma(pieces)] * 8
        + [dma(peers)] * 4
        + [dma((TILES,))] * 4
        + [dma((2,))] * 3,
        compiler_params=pltpu.CompilerParams(
            collective_id=0, has_side_effects=True, vmem_limit_bytes=62 * 2**20
        ),
        name="pipeline",
    )(source, matrix, inverse_in, inverse_out)


def compact(counts, rows):
    ends = jnp.cumsum(counts)
    at = jnp.arange(LIVE, dtype=jnp.int32)
    micro = jnp.sum((at[:, None] >= ends[None, :]).astype(jnp.int32), axis=1)
    begin = ends - counts
    slot = micro * ROWS + at - jnp.sum(
        jnp.where(micro[:, None] == jnp.arange(MICRO)[None, :], begin[None, :], 0), axis=1
    )
    chosen = (slot[:, None] == jnp.arange(TOK_DEV, dtype=jnp.int32)[None, :]).astype(jnp.bfloat16)
    return jnp.stack(
        [
            mm(chosen, rows[:, :HALF]).astype(jnp.bfloat16),
            mm(chosen, rows[:, HALF:]).astype(jnp.bfloat16),
        ]
    )


def shards(tokens, cotangent, live_counts, weight, inverse_in, inverse_out):
    section_here = lax.axis_index("section")
    source = compact(live_counts[0], jnp.where(section_here == 0, tokens, cotangent))
    update, owned_in, owned_out = run_pipeline(source, weight[0], inverse_in[0, 0], inverse_out[0])
    return (update[None], owned_in[None, None], owned_out[None, None])


def solution(mesh):
    in_specs = (
        P("dp", None),
        P("dp", None),
        P("dp", None),
        P("section", None, None),
        P("section", "dp", None, None),
        P("section", None, None, None),
    )
    out_specs = (
        P("section", "dp", None),
        P("section", "dp", None, None),
        P("section", "dp", None, None),
    )
    return jax.shard_map(shards, mesh=mesh, in_specs=in_specs, out_specs=out_specs, check_vma=False)
```

```python
import functools

import jax
import jax.numpy as jnp
from jax import lax
from jax.experimental import pallas as pl
from jax.experimental.pallas import tpu as pltpu
from jax.sharding import PartitionSpec as P

D = 3072
HALF = D // 2
BLOCK = 192
MICRO = 4
ROWS = 80
TOK_DEV = 320
LIVE = 240
NBLK = 16
PAIR = 2 * LIVE
CHUNK = 48
CHUNKS = PAIR // CHUNK
PIECES = 3
WIDTH = HALF // PIECES

C_ZERO = 0.7978845608028654
C_ONE = 0.044715
MESH = pl.DeviceIdType.MESH
RING = 4
QUAD = 4 * BLOCK
TWIN = 2 * BLOCK
CHIPS = 8
SHARE = CHUNKS // 2
SEEN = SHARE * CHIPS * CHUNK
TOKENS = 5120


def activate(value):
    return 0.5 * value * (1.0 + jnp.tanh(C_ZERO * (value + C_ONE * value * value * value)))


def slope(value):
    hyper = jnp.tanh(C_ZERO * (value + C_ONE * value * value * value))
    return 0.5 * (1.0 + hyper) + 0.5 * value * (1.0 - hyper * hyper) * C_ZERO * (
        1.0 + 3.0 * C_ONE * value * value
    )


def mm(a, b):
    return jnp.dot(a, b, preferred_element_type=jnp.float32)


def gram(a, b):
    return lax.dot_general(a, b, (((0,), (0,)), ((), ())), preferred_element_type=jnp.float32)


def pipeline(
    stages,
    source,
    weight,
    inv_in,
    inv_out,
    update,
    gram_in,
    gram_out,
    x_buf,
    s_buf,
    g_buf,
    slopes,
    h_send,
    w_fwd,
    w_bwd,
    w_raw,
    f_acc,
    b_acc,
    x_all,
    x_turned,
    s_all,
    e_send,
    e_recv,
    o_send,
    o_recv,
    p_raw,
    p_in,
    p_out,
    square,
    gi_send,
    gi_recv,
    go_send,
    go_recv,
    load_sem,
    init_send,
    init_recv,
    f_send_sem,
    f_recv_sem,
    b_send_sem,
    b_recv_sem,
    xs_send_sem,
    xs_recv_sem,
    ss_send_sem,
    ss_recv_sem,
    xa_send_sem,
    xa_recv_sem,
    sa_send_sem,
    sa_recv_sem,
    e_send_sem,
    e_recv_sem,
    o_send_sem,
    o_recv_sem,
    gi_sem,
    go_send_sem,
    go_recv_sem,
):
    stage = lax.axis_index("section")
    rank = lax.axis_index("dp")
    core = lax.rem(rank, 2)
    side = lax.rem(rank // 2, 2)
    ring = rank // 4
    upper = ring // 2
    quarter = 2 * lax.rem(ring, 2) + side
    chip = rank // 2
    sibling = {"dp": rank + 1 - 2 * core}
    last = stages - 1
    following = {"section": jnp.minimum(stage + 1, last)}
    previous = {"section": jnp.maximum(stage - 1, 0)}
    own_cols = pl.ds(pl.multiple_of(core * HALF, HALF), HALF)
    sib_cols = pl.ds(pl.multiple_of((1 - core) * HALF, HALF), HALF)

    def chip_at(d):
        return 2 * lax.rem(ring + d // 2, RING) + lax.rem(side + d, 2)

    def chip_before(d):
        return 2 * lax.rem(ring + RING - d // 2, RING) + lax.rem(side + d, 2)

    def go_rank(e):
        return quarter * 4 + upper * 2 + e

    def go_source(e):
        return (2 * side + ring // 2) * 4 + lax.rem(ring, 2) * 2 + e

    loads = (
        pltpu.make_async_copy(weight.at[own_cols, own_cols], w_fwd.at[0], load_sem.at[0]),
        pltpu.make_async_copy(weight.at[sib_cols, own_cols], w_fwd.at[1], load_sem.at[1]),
        pltpu.make_async_copy(weight.at[own_cols, sib_cols], w_raw, load_sem.at[2]),
    )
    for load in loads:
        load.start()

    barrier = pltpu.get_barrier_semaphore()

    def greet(device):
        pl.semaphore_signal(barrier, inc=1, device_id=device, device_id_type=MESH)

    greet(sibling)
    for d in range(1, CHIPS):
        greet({"dp": 2 * chip_at(d) + core})

    @pl.when(stage > 0)
    def _():
        greet(previous)

    @pl.when(stage < last)
    def _():
        greet(following)

    for e in range(2):

        @pl.when(go_source(e) != rank)
        def _():
            greet({"dp": go_source(e)})

    expected = CHIPS + (stage > 0).astype(jnp.int32) + (stage < last).astype(jnp.int32)
    for e in range(2):
        expected = expected + (go_rank(e) != rank).astype(jnp.int32)
    pl.semaphore_wait(barrier, expected)

    mine = pl.ds(pl.multiple_of(core * LIVE, 16), LIVE)

    def remote(src, dst, send, recv, device):
        return pltpu.make_async_remote_copy(
            src, dst, send, recv, device_id=device, device_id_type=MESH
        )

    @pl.when(stage == 0)
    def _():
        moves = (
            pltpu.make_async_copy(source.at[core], x_buf.at[0, mine], load_sem.at[3]),
            pltpu.make_async_copy(source.at[1 - core], x_buf.at[1, mine], load_sem.at[4]),
            remote(
                source.at[1 - core], x_buf.at[0, mine], init_send.at[0], init_recv.at[0], sibling
            ),
            remote(source.at[core], x_buf.at[1, mine], init_send.at[1], init_recv.at[1], sibling),
        )
        for move in moves:
            move.start()
        for move in moves:
            move.wait()

    @pl.when(stage == last)
    def _():
        moves = (
            pltpu.make_async_copy(source.at[core], g_buf.at[mine], load_sem.at[3]),
            remote(source.at[1 - core], g_buf.at[mine], init_send.at[0], init_recv.at[0], sibling),
        )
        for move in moves:
            move.start()
        for move in moves:
            move.wait()

    for load in loads:
        load.wait()

    def rows_of(k):
        return pl.ds(pl.multiple_of(k * CHUNK, 16), CHUNK)

    def cols_of(p):
        return pl.ds(p * WIDTH, WIDTH)

    def f_copy(k, p):
        at = (rows_of(k), cols_of(p))
        return remote(
            h_send.at[at], x_buf.at[(0,) + at], f_send_sem.at[k, p], f_recv_sem.at[k, p], following
        )

    def b_copy(k, p):
        at = (rows_of(k), cols_of(p))
        return remote(
            h_send.at[at], g_buf.at[at], b_send_sem.at[k, p], b_recv_sem.at[k, p], previous
        )

    def x_copy(k, p):
        at = (rows_of(k), cols_of(p))
        return remote(
            x_buf.at[(0,) + at], x_buf.at[(1,) + at], xs_send_sem.at[k, p], xs_recv_sem.at[k, p],
            sibling,
        )

    def s_copy(k, p):
        at = (rows_of(k), cols_of(p))
        return remote(
            s_buf.at[(0,) + at], s_buf.at[(1,) + at], ss_send_sem.at[k, p], ss_recv_sem.at[k, p],
            sibling,
        )

    def x_part(to, k):
        which = jnp.where(to // 4 == core, 0, 1)
        return x_buf.at[which, rows_of(k)]

    def s_part(to, k):
        which = jnp.where(lax.rem(to // 2, 2) == core, 0, 1)
        cols = pl.ds(pl.multiple_of(lax.rem(to, 2) * QUAD, QUAD), QUAD)
        return s_buf.at[which, rows_of(k), cols]

    def slot_of(i, who):
        return pl.ds(pl.multiple_of((i * CHIPS + who) * CHUNK, 16), CHUNK)

    def xa_send(k, d):
        i = k // 2
        return remote(
            x_part(chip_at(d), k), x_all.at[slot_of(i, chip)],
            xa_send_sem.at[i, d - 1], xa_recv_sem.at[i, d - 1], {"dp": 2 * chip_at(d) + core},
        )

    def xa_recv(i, d):
        here = x_all.at[slot_of(i, chip_before(d))]
        return remote(here, here, xa_send_sem.at[i, d - 1], xa_recv_sem.at[i, d - 1], sibling)

    def sa_send(k, d):
        i = k // 2
        return remote(
            s_part(chip_at(d), k), s_all.at[slot_of(i, chip)],
            sa_send_sem.at[i, d - 1], sa_recv_sem.at[i, d - 1], {"dp": 2 * chip_at(d) + core},
        )

    def sa_recv(i, d):
        here = s_all.at[slot_of(i, chip_before(d))]
        return remote(here, here, sa_send_sem.at[i, d - 1], sa_recv_sem.at[i, d - 1], sibling)

    end = cols_of(PIECES - 1)

    def forward_own(k):
        rows = rows_of(k)
        for p in range(PIECES):
            cols = cols_of(p)

            @pl.when(stage > 0)
            def _():
                f_copy(k, p).wait_recv()
                x_copy(k, p).start()

            term = mm(x_buf[0, rows, cols], w_fwd[0, cols, :])
            f_acc[...] = term if p == 0 else f_acc[...] + term

    def forward_rest(k):
        rows = rows_of(k)
        for p in range(PIECES):

            @pl.when(stage > 0)
            def _():
                x_copy(k, p).wait_recv()

            cols = cols_of(p)
            if p < PIECES - 1:
                f_acc[...] += mm(x_buf[1, rows, cols], w_fwd[1, cols, :])
        for p in range(PIECES):
            cols = cols_of(p)
            pre = f_acc[:, cols] + mm(x_buf[1, rows, end], w_fwd[1, end, cols])
            slopes[rows, cols] = pre

            @pl.when(stage < last)
            def _():
                h_send[rows, cols] = (
                    x_buf[0, rows, cols].astype(jnp.float32) + activate(pre)
                ).astype(jnp.bfloat16)
                f_copy(k, p).start()

    def forward_end(k):
        rows = rows_of(k)
        slopes[rows, :] = slope(slopes[rows, :])

        @pl.when(lax.rem(k, 2) == core)
        def _():
            for d in range(1, CHIPS):
                xa_send(k, d).start()
            which = jnp.where(upper == core, 0, 1)
            x_all[slot_of(k // 2, chip), :] = x_buf[which, rows, :]

    def backward_start(k):
        rows = rows_of(k)
        for p in range(PIECES):
            cols = cols_of(p)

            @pl.when(stage < last)
            def _():
                b_copy(k, p).wait_recv()

            s_buf[0, rows, cols] = (
                g_buf[rows, cols].astype(jnp.float32) * slopes[rows, cols]
            ).astype(jnp.bfloat16)
            s_copy(k, p).start()

    def backward_own(k):
        @pl.when(stage > 0)
        def _():
            rows = rows_of(k)
            b_acc[...] = mm(s_buf[0, rows, :], w_bwd[0])

    def backward_rest(k):
        rows = rows_of(k)
        for p in range(PIECES):
            s_copy(k, p).wait_recv()
            cols = cols_of(p)
            if p < PIECES - 1:

                @pl.when(stage > 0)
                def _():
                    b_acc[...] += mm(s_buf[1, rows, cols], w_bwd[1, cols, :])

        @pl.when(stage > 0)
        def _():
            @pl.when(stage < last)
            def _():
                for p in range(PIECES):
                    f_copy(k, p).wait_send()

            for p in range(PIECES):
                cols = cols_of(p)
                back = b_acc[:, cols] + mm(s_buf[1, rows, end], w_bwd[1, end, cols])
                h_send[rows, cols] = (
                    g_buf[rows, cols].astype(jnp.float32) + back
                ).astype(jnp.bfloat16)
                b_copy(k, p).start()

    def backward_end(k):
        @pl.when(lax.rem(k, 2) == core)
        def _():
            for d in range(1, CHIPS):
                sa_send(k, d).start()
            which = jnp.where(lax.rem(ring, 2) == core, 0, 1)
            cols = pl.ds(pl.multiple_of(side * QUAD, QUAD), QUAD)
            s_all[slot_of(k // 2, chip), :] = s_buf[which, rows_of(k), cols]

    turn_at = jnp.where(2 * stage + CHUNKS > 2 * last, 0, stage + CHUNKS)
    tile = 256

    def turn():
        @pl.when(stage > 0)
        def _():
            def step(i, carry):
                at = pl.ds(pl.multiple_of(i * tile, tile), tile)
                for j in range(HALF // tile):
                    to = pl.ds(j * tile, tile)
                    w_bwd[0, to, at] = w_fwd[0, at, to].T
                    w_bwd[1, to, at] = w_raw[at, to].T
                return carry

            lax.fori_loop(0, HALF // tile, step, 0)

        load = pltpu.make_async_copy(inv_in, p_raw.at[0], load_sem.at[0])
        load.start()
        load.wait()
        p_in[...] = p_raw[0].astype(jnp.bfloat16)
        p_out[...] = jnp.zeros_like(p_out)

        def step(i, carry):
            pair = pltpu.make_async_copy(inv_out.at[pl.ds(2 * i, 2)], p_raw, load_sem.at[0])
            pair.start()
            pair.wait()
            p_out[i, 0:BLOCK, 0:BLOCK] = p_raw[0].astype(jnp.bfloat16)
            p_out[i, BLOCK:TWIN, BLOCK:TWIN] = p_raw[1].astype(jnp.bfloat16)
            return carry

        lax.fori_loop(0, NBLK // 2, step, 0)

    gi_copy = remote(gi_send, gi_recv, gi_sem.at[0], gi_sem.at[1], sibling)

    def collect_x():
        def arrive(i, carry):
            for d in range(1, CHIPS):
                xa_recv(i, d).wait_recv()
            return carry

        lax.fori_loop(0, SHARE, arrive, 0)

        def turn_x(j, carry):
            cols = pl.ds(pl.multiple_of(j * tile, tile), tile)
            x_turned[cols, :] = x_all[:, cols].T
            return carry

        lax.fori_loop(0, HALF // tile, turn_x, 0)
        at = pl.ds(pl.multiple_of(quarter * TWIN, TWIN), TWIN)
        square[...] = mm(x_turned[at, :], x_all[:, at]) * (1.0 / TOKENS)
        for e in range(2):
            span = slice(e * BLOCK, (e + 1) * BLOCK)

            @pl.when(core == e)
            def _():
                gram_in[...] = square[span, span]

            @pl.when(core != e)
            def _():
                gi_send[...] = square[span, span]

        gi_copy.start()

    slots = 2 * last + CHUNKS + 1
    collect_at = jnp.where(stage == 0, CHUNKS, slots - stage)

    def slot(t, carry):
        @pl.when(t == turn_at)
        def _():
            turn()

        @pl.when(t == collect_at)
        def _():
            collect_x()

        kf = t - stage
        kb = t - (2 * last + 1 - stage)
        has_f = (kf >= 0) & (kf < CHUNKS)
        has_b = (kb >= 0) & (kb < CHUNKS)

        pl.when(has_b)(lambda: backward_start(kb))
        pl.when(has_f)(lambda: forward_own(kf))
        pl.when(has_b)(lambda: backward_own(kb))
        pl.when(has_f)(lambda: forward_rest(kf))
        pl.when(has_b)(lambda: backward_rest(kb))
        pl.when(has_f)(lambda: forward_end(kf))
        pl.when(has_b)(lambda: backward_end(kb))
        return carry

    lax.fori_loop(0, slots, slot, 0)

    def arrive(i, carry):
        for d in range(1, CHIPS):
            sa_recv(i, d).wait_recv()
        return carry

    lax.fori_loop(0, SHARE, arrive, 0)

    def block(j, parity):
        rows = pl.ds(pl.multiple_of((2 * j + parity) * BLOCK, 16), BLOCK)
        return mm(x_turned[rows, :], s_all[...])

    def e_copy(n):
        return remote(e_send.at[n], e_recv.at[n], e_send_sem.at[n], e_recv_sem.at[n], sibling)

    def o_copy(n, j):
        owner = {"dp": (2 * upper + j // 2) * 4 + lax.rem(j, 2) * 2 + core}
        return remote(
            o_send.at[n], o_recv.at[quarter], o_send_sem.at[n], o_recv_sem.at[quarter], owner
        )

    def reduce(n, carry):
        j = lax.rem(quarter + 1 + n, 4)
        e_send[n] = block(j, 1 - core).astype(jnp.bfloat16)
        e_copy(n).start()
        ours = block(j, core)
        e_copy(n).wait_recv()
        whole = (ours + e_recv[n].astype(jnp.float32)).astype(jnp.bfloat16)

        @pl.when(n < 3)
        def _():
            o_send[n] = whole
            o_copy(n, j).start()

        @pl.when(n == 3)
        def _():
            o_recv[quarter] = whole

        return carry

    lax.fori_loop(0, 4, reduce, 0)

    cols = pl.ds(pl.multiple_of(upper * TWIN, TWIN), TWIN)
    square[...] = gram(s_all[:, cols], s_all[:, cols]) * (1.0 / TOKENS)

    def go_remote(e, device):
        return remote(go_send.at[e], go_recv.at[core], go_send_sem.at[e], go_recv_sem.at[core], device)

    for e in range(2):
        span = slice(e * BLOCK, (e + 1) * BLOCK)
        go_send[e] = square[span, span]

        @pl.when(go_rank(e) == rank)
        def _():
            pltpu.make_async_copy(go_send.at[e], go_recv.at[core], go_recv_sem.at[core]).start()

        @pl.when(go_rank(e) != rank)
        def _():
            go_remote(e, {"dp": go_rank(e)}).start()

    def condition(n, carry):
        who = lax.rem(quarter + 4 - n, 4)

        @pl.when(n > 0)
        def _():
            here = o_recv.at[who]
            remote(here, here, o_send_sem.at[0], o_recv_sem.at[who], sibling).wait_recv()

        left = mm(p_in[...], o_recv[who]).astype(jnp.bfloat16)
        for j in range(2):
            right = mm(left[:, j * TWIN : (j + 1) * TWIN], p_out[2 * who + j])
            at = pl.ds(pl.multiple_of(who * QUAD + j * TWIN, TWIN), TWIN)
            update[:, at] = (right * (1.0 / TOKENS**0.5)).astype(jnp.bfloat16)
        return carry

    lax.fori_loop(0, 4, condition, 0)

    gi_copy.wait()
    gram_in[...] += gi_recv[...]
    for e in range(2):
        own = go_source(e) == rank

        @pl.when(own)
        def _():
            pltpu.make_async_copy(go_send.at[0], go_recv.at[e], go_recv_sem.at[e]).wait()

        @pl.when(jnp.logical_not(own))
        def _():
            here = go_recv.at[e]
            remote(here, here, go_send_sem.at[0], go_recv_sem.at[e], sibling).wait_recv()

    gram_out[...] = go_recv[0] + go_recv[1]

    def drain(k, carry):
        for p in range(PIECES):

            @pl.when((stage < last) & (stage == 0))
            def _():
                f_copy(k, p).wait_send()

            @pl.when(stage > 0)
            def _():
                x_copy(k, p).wait_send()
                b_copy(k, p).wait_send()

            s_copy(k, p).wait_send()

        @pl.when(lax.rem(k, 2) == core)
        def _():
            for d in range(1, CHIPS):
                xa_send(k, d).wait_send()
                sa_send(k, d).wait_send()

        return carry

    lax.fori_loop(0, CHUNKS, drain, 0)
    for n in range(4):
        e_copy(n).wait_send()
    for n in range(3):
        o_copy(n, lax.rem(quarter + 1 + n, 4)).wait_send()
    for e in range(2):

        @pl.when(go_rank(e) != rank)
        def _():
            go_remote(e, sibling).wait_send()


def run_pipeline(source, matrix, inverse_in, inverse_out):
    dma = pltpu.SemaphoreType.DMA
    any_space = pl.BlockSpec(memory_space=pl.ANY)
    in_vmem = pl.BlockSpec(memory_space=pltpu.VMEM)
    pieces = (CHUNKS, PIECES)
    peers = (SHARE, CHIPS - 1)
    bf16, f32 = jnp.bfloat16, jnp.float32
    return pl.pallas_call(
        functools.partial(pipeline, lax.axis_size("section")),
        out_shape=[
            jax.ShapeDtypeStruct((BLOCK, D), bf16),
            jax.ShapeDtypeStruct((BLOCK, BLOCK), f32),
            jax.ShapeDtypeStruct((BLOCK, BLOCK), f32),
        ],
        in_specs=[any_space] * 4,
        out_specs=[in_vmem] * 3,
        scratch_shapes=[
            pltpu.VMEM((2, PAIR, HALF), bf16),
            pltpu.VMEM((2, PAIR, HALF), bf16),
            pltpu.VMEM((PAIR, HALF), bf16),
            pltpu.VMEM((PAIR, HALF), f32),
            pltpu.VMEM((PAIR, HALF), bf16),
            pltpu.VMEM((2, HALF, HALF), bf16),
            pltpu.VMEM((2, HALF, HALF), bf16),
            pltpu.VMEM((HALF, HALF), bf16),
            pltpu.VMEM((CHUNK, HALF), f32),
            pltpu.VMEM((CHUNK, HALF), f32),
            pltpu.VMEM((SEEN, HALF), bf16),
            pltpu.VMEM((HALF, SEEN), bf16),
            pltpu.VMEM((SEEN, QUAD), bf16),
            pltpu.VMEM((4, BLOCK, QUAD), bf16),
            pltpu.VMEM((4, BLOCK, QUAD), bf16),
            pltpu.VMEM((3, BLOCK, QUAD), bf16),
            pltpu.VMEM((4, BLOCK, QUAD), bf16),
            pltpu.VMEM((2, BLOCK, BLOCK), f32),
            pltpu.VMEM((BLOCK, BLOCK), bf16),
            pltpu.VMEM((NBLK // 2, TWIN, TWIN), bf16),
            pltpu.VMEM((TWIN, TWIN), f32),
            pltpu.VMEM((BLOCK, BLOCK), f32),
            pltpu.VMEM((BLOCK, BLOCK), f32),
            pltpu.VMEM((2, BLOCK, BLOCK), f32),
            pltpu.VMEM((2, BLOCK, BLOCK), f32),
            dma((5,)),
            dma((2,)),
            dma((2,)),
        ]
        + [dma(pieces)] * 8
        + [dma(peers)] * 4
        + [dma((4,))] * 4
        + [dma((2,))] * 3,
        compiler_params=pltpu.CompilerParams(
            collective_id=0, has_side_effects=True, vmem_limit_bytes=62 * 2**20
        ),
        name="pipeline",
    )(source, matrix, inverse_in, inverse_out)


def compact(counts, rows):
    ends = jnp.cumsum(counts)
    at = jnp.arange(LIVE, dtype=jnp.int32)
    micro = jnp.sum((at[:, None] >= ends[None, :]).astype(jnp.int32), axis=1)
    begin = ends - counts
    slot = micro * ROWS + at - jnp.sum(
        jnp.where(micro[:, None] == jnp.arange(MICRO)[None, :], begin[None, :], 0), axis=1
    )
    chosen = (slot[:, None] == jnp.arange(TOK_DEV, dtype=jnp.int32)[None, :]).astype(jnp.bfloat16)
    return jnp.stack(
        [
            mm(chosen, rows[:, :HALF]).astype(jnp.bfloat16),
            mm(chosen, rows[:, HALF:]).astype(jnp.bfloat16),
        ]
    )


def shards(tokens, cotangent, live_counts, weight, inverse_in, inverse_out):
    section_here = lax.axis_index("section")
    source = compact(live_counts[0], jnp.where(section_here == 0, tokens, cotangent))
    update, owned_in, owned_out = run_pipeline(source, weight[0], inverse_in[0, 0], inverse_out[0])
    return (update[None], owned_in[None, None], owned_out[None, None])


def solution(mesh):
    in_specs = (
        P("dp", None),
        P("dp", None),
        P("dp", None),
        P("section", None, None),
        P("section", "dp", None, None),
        P("section", None, None, None),
    )
    out_specs = (
        P("section", "dp", None),
        P("section", "dp", None, None),
        P("section", "dp", None, None),
    )
    return jax.shard_map(shards, mesh=mesh, in_specs=in_specs, out_specs=out_specs, check_vma=False)
```

```python
import functools

import jax
import jax.numpy as jnp
from jax import lax
from jax.experimental import pallas as pl
from jax.experimental.pallas import tpu as pltpu
from jax.sharding import PartitionSpec as P

D = 3072
HALF = D // 2
BLOCK = 192
MICRO = 4
ROWS = 80
TOK_DEV = 320
LIVE = 240
NBLK = 16
PAIR = 2 * LIVE
CHUNK = 48
CHUNKS = PAIR // CHUNK
PIECES = 3
WIDTH = HALF // PIECES

C_ZERO = 0.7978845608028654
C_ONE = 0.044715
MESH = pl.DeviceIdType.MESH
RING = 4
QUAD = 4 * BLOCK
TWIN = 2 * BLOCK
CHIPS = 8
SHARE = CHUNKS // 2
AHEAD = 6
SEEN = SHARE * CHIPS * CHUNK
TOKENS = 5120


def activate(value):
    return 0.5 * value * (1.0 + jnp.tanh(C_ZERO * (value + C_ONE * value * value * value)))


def slope(value):
    hyper = jnp.tanh(C_ZERO * (value + C_ONE * value * value * value))
    return 0.5 * (1.0 + hyper) + 0.5 * value * (1.0 - hyper * hyper) * C_ZERO * (
        1.0 + 3.0 * C_ONE * value * value
    )


def mm(a, b):
    return jnp.dot(a, b, preferred_element_type=jnp.float32)


def gram(a, b):
    return lax.dot_general(a, b, (((0,), (0,)), ((), ())), preferred_element_type=jnp.float32)


def pipeline(
    stages,
    counts,
    tokens,
    cotangent,
    weight,
    inv_in,
    inv_out,
    update,
    gram_in,
    gram_out,
    x_buf,
    s_buf,
    g_buf,
    slopes,
    h_send,
    w_fwd,
    w_bwd,
    w_raw,
    acc,
    x_all,
    x_turned,
    s_all,
    e_send,
    e_recv,
    o_send,
    o_recv,
    p_raw,
    p_in,
    p_out,
    square,
    gi_send,
    gi_recv,
    go_send,
    go_recv,
    load_sem,
    init_send,
    init_recv,
    f_send_sem,
    f_recv_sem,
    b_send_sem,
    b_recv_sem,
    xs_send_sem,
    xs_recv_sem,
    ss_send_sem,
    ss_recv_sem,
    xa_send_sem,
    xa_recv_sem,
    sa_send_sem,
    sa_recv_sem,
    e_send_sem,
    e_recv_sem,
    o_send_sem,
    o_recv_sem,
    gi_sem,
    go_send_sem,
    go_recv_sem,
):
    stage = lax.axis_index("section")
    rank = lax.axis_index("dp")
    core = lax.rem(rank, 2)
    side = lax.rem(rank // 2, 2)
    ring = rank // 4
    upper = ring // 2
    quarter = 2 * lax.rem(ring, 2) + side
    chip = rank // 2
    sibling = {"dp": rank + 1 - 2 * core}
    last = stages - 1
    following = {"section": jnp.minimum(stage + 1, last)}
    previous = {"section": jnp.maximum(stage - 1, 0)}
    own_cols = pl.ds(pl.multiple_of(core * HALF, HALF), HALF)
    sib_cols = pl.ds(pl.multiple_of((1 - core) * HALF, HALF), HALF)

    def chip_at(d):
        return 2 * lax.rem(ring + d // 2, RING) + lax.rem(side + d, 2)

    def chip_before(d):
        return 2 * lax.rem(ring + RING - d // 2, RING) + lax.rem(side + d, 2)

    def go_rank(e):
        return quarter * 4 + upper * 2 + e

    def go_source(e):
        return (2 * side + ring // 2) * 4 + lax.rem(ring, 2) * 2 + e

    def staged(which):
        return x_turned.at[pl.ds(pl.multiple_of(which * TOK_DEV, 16), TOK_DEV), pl.ds(0, HALF)]

    def fetch(array):
        return [
            pltpu.make_async_copy(
                array.at[:, pl.ds(h * HALF, HALF)], staged(h), load_sem.at[3 + h]
            )
            for h in range(2)
        ]

    loads = (
        pltpu.make_async_copy(weight.at[own_cols, own_cols], w_fwd.at[0], load_sem.at[0]),
        pltpu.make_async_copy(weight.at[sib_cols, own_cols], w_fwd.at[1], load_sem.at[1]),
        pltpu.make_async_copy(weight.at[own_cols, sib_cols], w_raw, load_sem.at[2]),
    )
    for load in loads:
        load.start()

    @pl.when(stage == 0)
    def _():
        for move in fetch(tokens):
            move.start()

    @pl.when(stage == last)
    def _():
        for move in fetch(cotangent):
            move.start()

    barrier = pltpu.get_barrier_semaphore()

    def greet(device):
        pl.semaphore_signal(barrier, inc=1, device_id=device, device_id_type=MESH)

    greet(sibling)
    for d in range(1, CHIPS):
        greet({"dp": 2 * chip_at(d) + core})

    @pl.when(stage > 0)
    def _():
        greet(previous)

    @pl.when(stage < last)
    def _():
        greet(following)

    for e in range(2):

        @pl.when(go_source(e) != rank)
        def _():
            greet({"dp": go_source(e)})

    expected = CHIPS + (stage > 0).astype(jnp.int32) + (stage < last).astype(jnp.int32)
    for e in range(2):
        expected = expected + (go_rank(e) != rank).astype(jnp.int32)
    pl.semaphore_wait(barrier, expected)

    def remote(src, dst, send, recv, device):
        return pltpu.make_async_remote_copy(
            src, dst, send, recv, device_id=device, device_id_type=MESH
        )

    def rows_of(k):
        return pl.ds(pl.multiple_of(k * CHUNK, 16), CHUNK)

    def i_copy(k, h):
        return remote(
            x_buf.at[h, rows_of(k)], x_buf.at[1 - h, rows_of(k)],
            xs_send_sem.at[k, h], xs_recv_sem.at[k, h], sibling,
        )

    mine = pl.ds(pl.multiple_of(core * LIVE, 16), LIVE)

    def chosen():
        slots = lax.broadcasted_iota(jnp.int32, (LIVE, TOK_DEV), 1)
        places = jnp.full((LIVE, TOK_DEV), -1, jnp.int32)
        begin = jnp.int32(0)
        for m in range(MICRO):
            count = counts[m]
            slot = slots - m * ROWS
            places = jnp.where((slot >= 0) & (slot < count), begin + slot, places)
            begin = begin + count
        return (places == lax.broadcasted_iota(jnp.int32, (LIVE, TOK_DEV), 0)).astype(jnp.bfloat16)

    def picked(pick, which):
        return mm(pick, staged(which)[...]).astype(jnp.bfloat16)

    @pl.when(stage == 0)
    def _():
        for move in fetch(tokens):
            move.wait()
        pick = chosen()
        x_buf[0, mine, :] = picked(pick, core)
        x_buf[1, mine, :] = picked(pick, 1 - core)

        def give(n, carry):
            for h in range(2):
                i_copy(core * SHARE + n, h).start()
            return carry

        lax.fori_loop(0, SHARE, give, 0)

    @pl.when(stage == last)
    def _():
        for move in fetch(cotangent):
            move.wait()
        pick = chosen()
        g_buf[mine, :] = picked(pick, core)
        h_send[mine, :] = picked(pick, 1 - core)
        give = remote(h_send.at[mine], g_buf.at[mine], init_send.at[0], init_recv.at[0], sibling)
        give.start()
        give.wait()

    for load in loads:
        load.wait()

    def cols_of(p):
        return pl.ds(p * WIDTH, WIDTH)

    def f_copy(k, p):
        at = (rows_of(k), cols_of(p))
        return remote(
            h_send.at[at], x_buf.at[(0,) + at], f_send_sem.at[k, p], f_recv_sem.at[k, p], following
        )

    def b_copy(k, p):
        at = (rows_of(k), cols_of(p))
        return remote(
            h_send.at[at], g_buf.at[at], b_send_sem.at[k, p], b_recv_sem.at[k, p], previous
        )

    def x_copy(k, p):
        at = (rows_of(k), cols_of(p))
        return remote(
            x_buf.at[(0,) + at], x_buf.at[(1,) + at], xs_send_sem.at[k, p], xs_recv_sem.at[k, p],
            sibling,
        )

    def s_copy(k, p):
        at = (rows_of(k), cols_of(p))
        return remote(
            s_buf.at[(0,) + at], s_buf.at[(1,) + at], ss_send_sem.at[k, p], ss_recv_sem.at[k, p],
            sibling,
        )

    hold_x = (stage == last // 2) | (stage == last)
    hold_s = stage == last // 2 + 1

    def held(send):
        def step(i, carry):
            for d in range(1, CHIPS, 2):
                send(2 * i + core, d).start()
            return carry

        lax.fori_loop(0, SHARE, step, 0)

    def x_part(to, k):
        which = jnp.where(to // 4 == core, 0, 1)
        return x_buf.at[which, rows_of(k)]

    def s_part(to, k):
        which = jnp.where(lax.rem(to // 2, 2) == core, 0, 1)
        cols = pl.ds(pl.multiple_of(lax.rem(to, 2) * QUAD, QUAD), QUAD)
        return s_buf.at[which, rows_of(k), cols]

    def slot_of(i, who):
        return pl.ds(pl.multiple_of((i * CHIPS + who) * CHUNK, 16), CHUNK)

    def xa_send(k, d):
        i = k // 2
        return remote(
            x_part(chip_at(d), k), x_all.at[slot_of(i, chip)],
            xa_send_sem.at[i, d - 1], xa_recv_sem.at[i, d - 1], {"dp": 2 * chip_at(d) + core},
        )

    def xa_recv(i, d):
        here = x_all.at[slot_of(i, chip_before(d))]
        return remote(here, here, xa_send_sem.at[i, d - 1], xa_recv_sem.at[i, d - 1], sibling)

    def sa_send(k, d):
        i = k // 2
        return remote(
            s_part(chip_at(d), k), s_all.at[slot_of(i, chip)],
            sa_send_sem.at[i, d - 1], sa_recv_sem.at[i, d - 1], {"dp": 2 * chip_at(d) + core},
        )

    def sa_recv(i, d):
        here = s_all.at[slot_of(i, chip_before(d))]
        return remote(here, here, sa_send_sem.at[i, d - 1], sa_recv_sem.at[i, d - 1], sibling)

    end = cols_of(PIECES - 1)

    def forward_own(k):
        rows = rows_of(k)

        @pl.when((stage == 0) & (k // SHARE != core))
        def _():
            for h in range(2):
                i_copy(k, h).wait_recv()

        for p in range(PIECES):
            cols = cols_of(p)

            @pl.when(stage > 0)
            def _():
                f_copy(k, p).wait_recv()
                x_copy(k, p).start()

            term = mm(x_buf[0, rows, cols], w_fwd[0, cols, :])
            acc[...] = term if p == 0 else acc[...] + term

    def forward_rest(k):
        rows = rows_of(k)
        for p in range(PIECES):

            @pl.when(stage > 0)
            def _():
                x_copy(k, p).wait_recv()

            cols = cols_of(p)
            if p < PIECES - 1:
                acc[...] += mm(x_buf[1, rows, cols], w_fwd[1, cols, :])
        for p in range(PIECES):
            cols = cols_of(p)
            pre = acc[:, cols] + mm(x_buf[1, rows, end], w_fwd[1, end, cols])
            slopes[rows, cols] = pre

            @pl.when(stage < last)
            def _():
                h_send[rows, cols] = (
                    x_buf[0, rows, cols].astype(jnp.float32) + activate(pre)
                ).astype(jnp.bfloat16)
                f_copy(k, p).start()

    def forward_end(k):
        rows = rows_of(k)
        slopes[rows, :] = slope(slopes[rows, :])

        @pl.when(lax.rem(k, 2) == core)
        def _():
            for d in range(2, CHIPS, 2):
                xa_send(k, d).start()

            @pl.when(jnp.logical_not(hold_x))
            def _():
                for d in range(1, CHIPS, 2):
                    xa_send(k, d).start()

            which = jnp.where(upper == core, 0, 1)
            x_all[slot_of(k // 2, chip), :] = x_buf[which, rows, :]

    def backward_start(k):
        rows = rows_of(k)
        for p in range(PIECES):
            cols = cols_of(p)

            @pl.when(stage < last)
            def _():
                b_copy(k, p).wait_recv()

            s_buf[0, rows, cols] = (
                g_buf[rows, cols].astype(jnp.float32) * slopes[rows, cols]
            ).astype(jnp.bfloat16)
            s_copy(k, p).start()

    def backward_own(k):
        @pl.when(stage > 0)
        def _():
            rows = rows_of(k)
            acc[...] = mm(s_buf[0, rows, :], w_bwd[0])

    def backward_rest(k):
        rows = rows_of(k)
        for p in range(PIECES):
            s_copy(k, p).wait_recv()
            cols = cols_of(p)
            if p < PIECES - 1:

                @pl.when(stage > 0)
                def _():
                    acc[...] += mm(s_buf[1, rows, cols], w_bwd[1, cols, :])

        @pl.when(stage > 0)
        def _():
            @pl.when(stage < last)
            def _():
                for p in range(PIECES):
                    f_copy(k, p).wait_send()

            for p in range(PIECES):
                cols = cols_of(p)
                back = acc[:, cols] + mm(s_buf[1, rows, end], w_bwd[1, end, cols])
                h_send[rows, cols] = (
                    g_buf[rows, cols].astype(jnp.float32) + back
                ).astype(jnp.bfloat16)
                b_copy(k, p).start()

    def backward_end(k):
        @pl.when(lax.rem(k, 2) == core)
        def _():
            for d in range(2, CHIPS, 2):
                sa_send(k, d).start()

            @pl.when(jnp.logical_not(hold_s))
            def _():
                for d in range(1, CHIPS, 2):
                    sa_send(k, d).start()

            which = jnp.where(lax.rem(ring, 2) == core, 0, 1)
            cols = pl.ds(pl.multiple_of(side * QUAD, QUAD), QUAD)
            s_all[slot_of(k // 2, chip), :] = s_buf[which, rows_of(k), cols]

    tile = 256

    def turn():
        @pl.when(stage > 0)
        def _():
            def step(i, carry):
                at = pl.ds(pl.multiple_of(i * tile, tile), tile)
                for j in range(HALF // tile):
                    to = pl.ds(j * tile, tile)
                    w_bwd[0, to, at] = w_fwd[0, at, to].T
                    w_bwd[1, to, at] = w_raw[at, to].T
                return carry

            lax.fori_loop(0, HALF // tile, step, 0)

        load = pltpu.make_async_copy(inv_in, p_raw.at[0], load_sem.at[0])
        load.start()
        load.wait()
        p_in[...] = p_raw[0].astype(jnp.bfloat16)
        p_out[...] = jnp.zeros_like(p_out)

        def step(i, carry):
            pair = pltpu.make_async_copy(inv_out.at[pl.ds(2 * i, 2)], p_raw, load_sem.at[0])
            pair.start()
            pair.wait()
            p_out[i, 0:BLOCK, 0:BLOCK] = p_raw[0].astype(jnp.bfloat16)
            p_out[i, BLOCK:TWIN, BLOCK:TWIN] = p_raw[1].astype(jnp.bfloat16)
            return carry

        lax.fori_loop(0, NBLK // 2, step, 0)

    gi_copy = remote(gi_send, gi_recv, gi_sem.at[0], gi_sem.at[1], sibling)

    def collect_x():
        def arrive(i, carry):
            for d in range(1, CHIPS):
                xa_recv(i, d).wait_recv()
            return carry

        lax.fori_loop(0, SHARE, arrive, 0)

        def turn_x(j, carry):
            cols = pl.ds(pl.multiple_of(j * tile, tile), tile)
            x_turned[cols, :] = x_all[:, cols].T
            return carry

        lax.fori_loop(0, HALF // tile, turn_x, 0)
        at = pl.ds(pl.multiple_of(quarter * TWIN, TWIN), TWIN)
        square[...] = mm(x_turned[at, :], x_all[:, at]) * (1.0 / TOKENS)
        for e in range(2):
            span = slice(e * BLOCK, (e + 1) * BLOCK)

            @pl.when(core == e)
            def _():
                gram_in[...] = square[span, span]

            @pl.when(core != e)
            def _():
                gi_send[...] = square[span, span]

        gi_copy.start()

    ahead = jnp.where(stage == last, 1, jnp.where(stage == last - 1, AHEAD, CHUNKS))

    def slot(t, carry):
        @pl.when(t < CHUNKS)
        def _():
            forward_own(t)
            forward_rest(t)
            forward_end(t)

        @pl.when((t == CHUNKS - 1) & hold_x)
        def _():
            held(xa_send)

        @pl.when((t == CHUNKS - 1) & (2 * stage + CHUNKS <= 2 * last))
        def _():
            turn()

        @pl.when((t == CHUNKS - 1) & (stage == 0))
        def _():
            collect_x()

        @pl.when(t >= ahead - 1)
        def _():
            kb = t - (ahead - 1)
            backward_start(kb)
            backward_own(kb)
            backward_rest(kb)
            backward_end(kb)

        return carry

    @pl.when(2 * stage + CHUNKS > 2 * last)
    def _():
        turn()

    lax.fori_loop(0, CHUNKS + ahead - 1, slot, 0)

    @pl.when(hold_s)
    def _():
        held(sa_send)

    @pl.when(stage > 0)
    def _():
        collect_x()

    def arrive(i, carry):
        for d in range(1, CHIPS):
            sa_recv(i, d).wait_recv()
        return carry

    lax.fori_loop(0, SHARE, arrive, 0)

    def block(j, parity):
        rows = pl.ds(pl.multiple_of((2 * j + parity) * BLOCK, 16), BLOCK)
        return mm(x_turned[rows, :], s_all[...])

    def e_copy(n):
        return remote(e_send.at[n], e_recv.at[n], e_send_sem.at[n], e_recv_sem.at[n], sibling)

    def o_copy(n, j):
        owner = {"dp": (2 * upper + j // 2) * 4 + lax.rem(j, 2) * 2 + core}
        return remote(
            o_send.at[n], o_recv.at[quarter], o_send_sem.at[n], o_recv_sem.at[quarter], owner
        )

    def reduce(n, carry):
        j = lax.rem(quarter + 1 + n, 4)
        e_send[n] = block(j, 1 - core).astype(jnp.bfloat16)
        e_copy(n).start()
        ours = block(j, core)
        e_copy(n).wait_recv()
        whole = (ours + e_recv[n].astype(jnp.float32)).astype(jnp.bfloat16)

        @pl.when(n < 3)
        def _():
            o_send[n] = whole
            o_copy(n, j).start()

        @pl.when(n == 3)
        def _():
            o_recv[quarter] = whole

        return carry

    lax.fori_loop(0, 4, reduce, 0)

    cols = pl.ds(pl.multiple_of(upper * TWIN, TWIN), TWIN)
    square[...] = gram(s_all[:, cols], s_all[:, cols]) * (1.0 / TOKENS)

    def go_remote(e, device):
        return remote(go_send.at[e], go_recv.at[core], go_send_sem.at[e], go_recv_sem.at[core], device)

    for e in range(2):
        span = slice(e * BLOCK, (e + 1) * BLOCK)
        go_send[e] = square[span, span]

        @pl.when(go_rank(e) == rank)
        def _():
            pltpu.make_async_copy(go_send.at[e], go_recv.at[core], go_recv_sem.at[core]).start()

        @pl.when(go_rank(e) != rank)
        def _():
            go_remote(e, {"dp": go_rank(e)}).start()

    def condition(n, carry):
        who = lax.rem(quarter + 4 - n, 4)

        @pl.when(n > 0)
        def _():
            here = o_recv.at[who]
            remote(here, here, o_send_sem.at[0], o_recv_sem.at[who], sibling).wait_recv()

        left = mm(p_in[...], o_recv[who]).astype(jnp.bfloat16)
        for j in range(2):
            right = mm(left[:, j * TWIN : (j + 1) * TWIN], p_out[2 * who + j])
            at = pl.ds(pl.multiple_of(who * QUAD + j * TWIN, TWIN), TWIN)
            update[:, at] = (right * (1.0 / TOKENS**0.5)).astype(jnp.bfloat16)
        return carry

    lax.fori_loop(0, 4, condition, 0)

    gi_copy.wait()
    gram_in[...] += gi_recv[...]
    for e in range(2):
        own = go_source(e) == rank

        @pl.when(own)
        def _():
            pltpu.make_async_copy(go_send.at[0], go_recv.at[e], go_recv_sem.at[e]).wait()

        @pl.when(jnp.logical_not(own))
        def _():
            here = go_recv.at[e]
            remote(here, here, go_send_sem.at[0], go_recv_sem.at[e], sibling).wait_recv()

    gram_out[...] = go_recv[0] + go_recv[1]

    def drain(k, carry):
        for p in range(PIECES):

            @pl.when((stage < last) & (stage == 0))
            def _():
                f_copy(k, p).wait_send()

            @pl.when(stage > 0)
            def _():
                x_copy(k, p).wait_send()
                b_copy(k, p).wait_send()

            s_copy(k, p).wait_send()

        @pl.when((stage == 0) & (k // SHARE == core))
        def _():
            for h in range(2):
                i_copy(k, h).wait_send()

        @pl.when(lax.rem(k, 2) == core)
        def _():
            for d in range(1, CHIPS):
                xa_send(k, d).wait_send()
                sa_send(k, d).wait_send()

        return carry

    lax.fori_loop(0, CHUNKS, drain, 0)
    for n in range(4):
        e_copy(n).wait_send()
    for n in range(3):
        o_copy(n, lax.rem(quarter + 1 + n, 4)).wait_send()
    for e in range(2):

        @pl.when(go_rank(e) != rank)
        def _():
            go_remote(e, sibling).wait_send()


def run_pipeline(counts, tokens, cotangent, matrix, inverse_in, inverse_out):
    dma = pltpu.SemaphoreType.DMA
    any_space = pl.BlockSpec(memory_space=pl.ANY)
    in_vmem = pl.BlockSpec(memory_space=pltpu.VMEM)
    pieces = (CHUNKS, PIECES)
    peers = (SHARE, CHIPS - 1)
    bf16, f32 = jnp.bfloat16, jnp.float32
    return pl.pallas_call(
        functools.partial(pipeline, lax.axis_size("section")),
        out_shape=[
            jax.ShapeDtypeStruct((BLOCK, D), bf16),
            jax.ShapeDtypeStruct((BLOCK, BLOCK), f32),
            jax.ShapeDtypeStruct((BLOCK, BLOCK), f32),
        ],
        in_specs=[pl.BlockSpec(memory_space=pltpu.SMEM)] + [any_space] * 5,
        out_specs=[in_vmem] * 3,
        scratch_shapes=[
            pltpu.VMEM((2, PAIR, HALF), bf16),
            pltpu.VMEM((2, PAIR, HALF), bf16),
            pltpu.VMEM((PAIR, HALF), bf16),
            pltpu.VMEM((PAIR, HALF), f32),
            pltpu.VMEM((PAIR, HALF), bf16),
            pltpu.VMEM((2, HALF, HALF), bf16),
            pltpu.VMEM((2, HALF, HALF), bf16),
            pltpu.VMEM((HALF, HALF), bf16),
            pltpu.VMEM((CHUNK, HALF), f32),
            pltpu.VMEM((SEEN, HALF), bf16),
            pltpu.VMEM((HALF, SEEN), bf16),
            pltpu.VMEM((SEEN, QUAD), bf16),
            pltpu.VMEM((4, BLOCK, QUAD), bf16),
            pltpu.VMEM((4, BLOCK, QUAD), bf16),
            pltpu.VMEM((3, BLOCK, QUAD), bf16),
            pltpu.VMEM((4, BLOCK, QUAD), bf16),
            pltpu.VMEM((2, BLOCK, BLOCK), f32),
            pltpu.VMEM((BLOCK, BLOCK), bf16),
            pltpu.VMEM((NBLK // 2, TWIN, TWIN), bf16),
            pltpu.VMEM((TWIN, TWIN), f32),
            pltpu.VMEM((BLOCK, BLOCK), f32),
            pltpu.VMEM((BLOCK, BLOCK), f32),
            pltpu.VMEM((2, BLOCK, BLOCK), f32),
            pltpu.VMEM((2, BLOCK, BLOCK), f32),
            dma((5,)),
            dma((1,)),
            dma((1,)),
        ]
        + [dma(pieces)] * 8
        + [dma(peers)] * 4
        + [dma((4,))] * 4
        + [dma((2,))] * 3,
        compiler_params=pltpu.CompilerParams(
            collective_id=0, has_side_effects=True, vmem_limit_bytes=62 * 2**20
        ),
        name="pipeline",
    )(counts, tokens, cotangent, matrix, inverse_in, inverse_out)


def shards(tokens, cotangent, live_counts, weight, inverse_in, inverse_out):
    update, owned_in, owned_out = run_pipeline(
        live_counts[0], tokens, cotangent, weight[0], inverse_in[0, 0], inverse_out[0]
    )
    return (update[None], owned_in[None, None], owned_out[None, None])


def solution(mesh):
    in_specs = (
        P("dp", None),
        P("dp", None),
        P("dp", None),
        P("section", None, None),
        P("section", "dp", None, None),
        P("section", None, None, None),
    )
    out_specs = (
        P("section", "dp", None),
        P("section", "dp", None, None),
        P("section", "dp", None, None),
    )
    return jax.shard_map(shards, mesh=mesh, in_specs=in_specs, out_specs=out_specs, check_vma=False)
```

```python
import functools

import jax
import jax.numpy as jnp
from jax import lax
from jax.experimental import pallas as pl
from jax.experimental.pallas import tpu as pltpu
from jax.sharding import PartitionSpec as P

D = 3072
HALF = D // 2
BLOCK = 192
MICRO = 4
ROWS = 80
TOK_DEV = 320
LIVE = 240
NBLK = 16
PAIR = 2 * LIVE
CHUNK = 48
CHUNKS = PAIR // CHUNK
PIECES = 2
WIDTH = HALF // PIECES

C_ZERO = 0.7978845608028654
C_ONE = 0.044715
MESH = pl.DeviceIdType.MESH
RING = 4
QUAD = 4 * BLOCK
TWIN = 2 * BLOCK
CHIPS = 8
SHARE = CHUNKS // 2
AHEAD = 6
HELD = 3
DIRECT = (1, 5)
INDIRECT = (3, 7)
SEEN = SHARE * CHIPS * CHUNK
TOKENS = 5120


def activate(value):
    return 0.5 * value * (1.0 + jnp.tanh(C_ZERO * (value + C_ONE * value * value * value)))


def slope(value):
    hyper = jnp.tanh(C_ZERO * (value + C_ONE * value * value * value))
    return 0.5 * (1.0 + hyper) + 0.5 * value * (1.0 - hyper * hyper) * C_ZERO * (
        1.0 + 3.0 * C_ONE * value * value
    )


def mm(a, b):
    return jnp.dot(a, b, preferred_element_type=jnp.float32)


def gram(a, b):
    return lax.dot_general(a, b, (((0,), (0,)), ((), ())), preferred_element_type=jnp.float32)


def pipeline(
    stages,
    counts,
    tokens,
    cotangent,
    weight,
    inv_in,
    inv_out,
    update,
    gram_in,
    gram_out,
    x_buf,
    s_buf,
    g_buf,
    slopes,
    h_send,
    w_fwd,
    w_bwd,
    w_raw,
    acc,
    x_all,
    x_turned,
    s_all,
    e_send,
    e_recv,
    o_send,
    o_recv,
    p_raw,
    p_in,
    p_out,
    square,
    gi_send,
    gi_recv,
    go_send,
    go_recv,
    load_sem,
    init_send,
    init_recv,
    f_send_sem,
    f_recv_sem,
    b_send_sem,
    b_recv_sem,
    xs_send_sem,
    xs_recv_sem,
    ss_send_sem,
    ss_recv_sem,
    xa_send_sem,
    xa_recv_sem,
    xp_send_sem,
    sa_send_sem,
    sa_recv_sem,
    e_send_sem,
    e_recv_sem,
    o_send_sem,
    o_recv_sem,
    gi_sem,
    go_send_sem,
    go_recv_sem,
):
    stage = lax.axis_index("section")
    rank = lax.axis_index("dp")
    core = lax.rem(rank, 2)
    side = lax.rem(rank // 2, 2)
    ring = rank // 4
    upper = ring // 2
    quarter = 2 * lax.rem(ring, 2) + side
    chip = rank // 2
    sibling = {"dp": rank + 1 - 2 * core}
    last = stages - 1
    following = {"section": jnp.minimum(stage + 1, last)}
    previous = {"section": jnp.maximum(stage - 1, 0)}
    own_cols = pl.ds(pl.multiple_of(core * HALF, HALF), HALF)
    sib_cols = pl.ds(pl.multiple_of((1 - core) * HALF, HALF), HALF)

    def chip_at(d):
        return 2 * lax.rem(ring + d // 2, RING) + lax.rem(side + d, 2)

    def chip_before(d):
        return 2 * lax.rem(ring + RING - d // 2, RING) + lax.rem(side + d, 2)

    def go_rank(e):
        return quarter * 4 + upper * 2 + e

    def go_source(e):
        return (2 * side + ring // 2) * 4 + lax.rem(ring, 2) * 2 + e

    def staged(which):
        return x_turned.at[pl.ds(pl.multiple_of(which * TOK_DEV, 16), TOK_DEV), pl.ds(0, HALF)]

    def fetch(array):
        return [
            pltpu.make_async_copy(
                array.at[:, pl.ds(h * HALF, HALF)], staged(h), load_sem.at[3 + h]
            )
            for h in range(2)
        ]

    loads = (
        pltpu.make_async_copy(weight.at[own_cols, own_cols], w_fwd.at[0], load_sem.at[0]),
        pltpu.make_async_copy(weight.at[sib_cols, own_cols], w_fwd.at[1], load_sem.at[1]),
        pltpu.make_async_copy(weight.at[own_cols, sib_cols], w_raw, load_sem.at[2]),
    )
    for load in loads:
        load.start()

    @pl.when(stage == 0)
    def _():
        for move in fetch(tokens):
            move.start()

    @pl.when(stage == last)
    def _():
        for move in fetch(cotangent):
            move.start()

    barrier = pltpu.get_barrier_semaphore()

    def greet(device):
        pl.semaphore_signal(barrier, inc=1, device_id=device, device_id_type=MESH)

    greet(sibling)
    for d in range(1, CHIPS):
        greet({"dp": 2 * chip_at(d) + core})

    @pl.when(stage > 0)
    def _():
        greet(previous)

    @pl.when(stage < last)
    def _():
        greet(following)

    for e in range(2):

        @pl.when(go_source(e) != rank)
        def _():
            greet({"dp": go_source(e)})

    expected = CHIPS + (stage > 0).astype(jnp.int32) + (stage < last).astype(jnp.int32)
    for e in range(2):
        expected = expected + (go_rank(e) != rank).astype(jnp.int32)
    pl.semaphore_wait(barrier, expected)

    def remote(src, dst, send, recv, device):
        return pltpu.make_async_remote_copy(
            src, dst, send, recv, device_id=device, device_id_type=MESH
        )

    def rows_of(k):
        return pl.ds(pl.multiple_of(k * CHUNK, 16), CHUNK)

    def i_copy(k, h):
        return remote(
            x_buf.at[h, rows_of(k)], x_buf.at[1 - h, rows_of(k)],
            xs_send_sem.at[k, h], xs_recv_sem.at[k, h], sibling,
        )

    mine = pl.ds(pl.multiple_of(core * LIVE, 16), LIVE)

    def chosen():
        slots = lax.broadcasted_iota(jnp.int32, (LIVE, TOK_DEV), 1)
        places = jnp.full((LIVE, TOK_DEV), -1, jnp.int32)
        begin = jnp.int32(0)
        for m in range(MICRO):
            count = counts[m]
            slot = slots - m * ROWS
            places = jnp.where((slot >= 0) & (slot < count), begin + slot, places)
            begin = begin + count
        return (places == lax.broadcasted_iota(jnp.int32, (LIVE, TOK_DEV), 0)).astype(jnp.bfloat16)

    def picked(pick, which):
        return mm(pick, staged(which)[...]).astype(jnp.bfloat16)

    @pl.when(stage == 0)
    def _():
        for move in fetch(tokens):
            move.wait()
        pick = chosen()
        x_buf[0, mine, :] = picked(pick, core)
        x_buf[1, mine, :] = picked(pick, 1 - core)

        def give(n, carry):
            for h in range(2):
                i_copy(core * SHARE + n, h).start()
            return carry

        lax.fori_loop(0, SHARE, give, 0)

    @pl.when(stage == last)
    def _():
        for move in fetch(cotangent):
            move.wait()
        pick = chosen()
        g_buf[mine, :] = picked(pick, core)
        h_send[mine, :] = picked(pick, 1 - core)
        give = remote(h_send.at[mine], g_buf.at[mine], init_send.at[0], init_recv.at[0], sibling)
        give.start()
        give.wait()

    for load in loads:
        load.wait()

    def cols_of(p):
        return pl.ds(p * WIDTH, WIDTH)

    def f_copy(k, p):
        at = (rows_of(k), cols_of(p))
        return remote(
            h_send.at[at], x_buf.at[(0,) + at], f_send_sem.at[k, p], f_recv_sem.at[k, p], following
        )

    def b_copy(k, p):
        at = (rows_of(k), cols_of(p))
        return remote(
            h_send.at[at], g_buf.at[at], b_send_sem.at[k, p], b_recv_sem.at[k, p], previous
        )

    def x_copy(k, p):
        at = (rows_of(k), cols_of(p))
        return remote(
            x_buf.at[(0,) + at], x_buf.at[(1,) + at], xs_send_sem.at[k, p], xs_recv_sem.at[k, p],
            sibling,
        )

    def s_copy(k, p):
        at = (rows_of(k), cols_of(p))
        return remote(
            s_buf.at[(0,) + at], s_buf.at[(1,) + at], ss_send_sem.at[k, p], ss_recv_sem.at[k, p],
            sibling,
        )

    hold_x = stage == last // 2
    hold_s = stage == last // 2 + 1
    passing = hold_x | hold_s

    def x_part(to, k):
        which = jnp.where(to // 4 == core, 0, 1)
        return x_buf.at[which, rows_of(k)]

    def s_part(to, k):
        which = jnp.where(lax.rem(to // 2, 2) == core, 0, 1)
        cols = pl.ds(pl.multiple_of(lax.rem(to, 2) * QUAD, QUAD), QUAD)
        return s_buf.at[which, rows_of(k), cols]

    def slot_of(i, who):
        return pl.ds(pl.multiple_of((i * CHIPS + who) * CHUNK, 16), CHUNK)

    def xa_send(k, d):
        i = k // 2
        return remote(
            x_part(chip_at(d), k), x_all.at[slot_of(i, chip)],
            xa_send_sem.at[i, d - 1], xa_recv_sem.at[i, d - 1], {"dp": 2 * chip_at(d) + core},
        )

    def xa_recv(i, d):
        here = x_all.at[slot_of(i, chip_before(d))]
        return remote(here, here, xa_send_sem.at[i, d - 1], xa_recv_sem.at[i, d - 1], sibling)

    def pass_on(i, d):
        here = x_all.at[slot_of(i, chip_before(d))]
        beside = ring + 1 - 2 * lax.rem(ring, 2)
        away = lax.rem(beside - ring + d // 2 + RING, RING)
        return remote(
            here, here, xp_send_sem.at[i, d // 4], xa_recv_sem.at[i, 2 * away],
            {"dp": 4 * beside + lax.rem(rank, 4)},
        )

    def pass_all():
        def step(i, carry):
            for d in DIRECT:
                xa_recv(i, d).wait_recv()
                pass_on(i, d).start()
            return carry

        lax.fori_loop(0, SHARE, step, 0)

    def sa_send(k, d):
        i = k // 2
        return remote(
            s_part(chip_at(d), k), s_all.at[slot_of(i, chip)],
            sa_send_sem.at[i, d - 1], sa_recv_sem.at[i, d - 1], {"dp": 2 * chip_at(d) + core},
        )

    def sa_recv(i, d):
        here = s_all.at[slot_of(i, chip_before(d))]
        return remote(here, here, sa_send_sem.at[i, d - 1], sa_recv_sem.at[i, d - 1], sibling)

    end = cols_of(PIECES - 1)

    def forward_own(k):
        rows = rows_of(k)

        @pl.when((stage == 0) & (k // SHARE != core))
        def _():
            for h in range(2):
                i_copy(k, h).wait_recv()

        for p in range(PIECES):
            cols = cols_of(p)

            @pl.when(stage > 0)
            def _():
                f_copy(k, p).wait_recv()
                x_copy(k, p).start()

            term = mm(x_buf[0, rows, cols], w_fwd[0, cols, :])
            acc[...] = term if p == 0 else acc[...] + term

    def forward_rest(k):
        rows = rows_of(k)
        for p in range(PIECES):

            @pl.when(stage > 0)
            def _():
                x_copy(k, p).wait_recv()

            cols = cols_of(p)
            if p < PIECES - 1:
                acc[...] += mm(x_buf[1, rows, cols], w_fwd[1, cols, :])
        for p in range(PIECES):
            cols = cols_of(p)
            pre = acc[:, cols] + mm(x_buf[1, rows, end], w_fwd[1, end, cols])
            slopes[rows, cols] = pre

            @pl.when(stage < last)
            def _():
                h_send[rows, cols] = (
                    x_buf[0, rows, cols].astype(jnp.float32) + activate(pre)
                ).astype(jnp.bfloat16)
                f_copy(k, p).start()

    def forward_end(k):
        rows = rows_of(k)
        slopes[rows, :] = slope(slopes[rows, :])

        @pl.when(lax.rem(k, 2) == core)
        def _():
            for d in range(2, CHIPS, 2):
                xa_send(k, d).start()

            @pl.when(jnp.logical_not(hold_x))
            def _():
                for d in DIRECT:
                    xa_send(k, d).start()

            @pl.when(jnp.logical_not(passing))
            def _():
                for d in INDIRECT:
                    xa_send(k, d).start()

            which = jnp.where(upper == core, 0, 1)
            x_all[slot_of(k // 2, chip), :] = x_buf[which, rows, :]

    def backward_start(k):
        rows = rows_of(k)
        for p in range(PIECES):
            cols = cols_of(p)

            @pl.when(stage < last)
            def _():
                b_copy(k, p).wait_recv()

            s_buf[0, rows, cols] = (
                g_buf[rows, cols].astype(jnp.float32) * slopes[rows, cols]
            ).astype(jnp.bfloat16)
            s_copy(k, p).start()

    def backward_own(k):
        @pl.when(stage > 0)
        def _():
            rows = rows_of(k)
            acc[...] = mm(s_buf[0, rows, :], w_bwd[0])

    def backward_rest(k):
        rows = rows_of(k)
        for p in range(PIECES):
            s_copy(k, p).wait_recv()
            cols = cols_of(p)
            if p < PIECES - 1:

                @pl.when(stage > 0)
                def _():
                    acc[...] += mm(s_buf[1, rows, cols], w_bwd[1, cols, :])

        @pl.when(stage > 0)
        def _():
            @pl.when(stage < last)
            def _():
                for p in range(PIECES):
                    f_copy(k, p).wait_send()

            for p in range(PIECES):
                cols = cols_of(p)
                back = acc[:, cols] + mm(s_buf[1, rows, end], w_bwd[1, end, cols])
                h_send[rows, cols] = (
                    g_buf[rows, cols].astype(jnp.float32) + back
                ).astype(jnp.bfloat16)
                b_copy(k, p).start()

    def backward_end(k):
        @pl.when(lax.rem(k, 2) == core)
        def _():
            for d in range(2, CHIPS, 2):
                sa_send(k, d).start()

            @pl.when(jnp.logical_not(hold_s) | (k < HELD))
            def _():
                for d in range(1, CHIPS, 2):
                    sa_send(k, d).start()

            which = jnp.where(lax.rem(ring, 2) == core, 0, 1)
            cols = pl.ds(pl.multiple_of(side * QUAD, QUAD), QUAD)
            s_all[slot_of(k // 2, chip), :] = s_buf[which, rows_of(k), cols]

    tile = 256

    def turn():
        @pl.when(stage > 0)
        def _():
            def step(i, carry):
                at = pl.ds(pl.multiple_of(i * tile, tile), tile)
                for j in range(HALF // tile):
                    to = pl.ds(j * tile, tile)
                    w_bwd[0, to, at] = w_fwd[0, at, to].T
                    w_bwd[1, to, at] = w_raw[at, to].T
                return carry

            lax.fori_loop(0, HALF // tile, step, 0)

        load = pltpu.make_async_copy(inv_in, p_raw.at[0], load_sem.at[0])
        load.start()
        load.wait()
        p_in[...] = p_raw[0].astype(jnp.bfloat16)
        p_out[...] = jnp.zeros_like(p_out)

        def step(i, carry):
            pair = pltpu.make_async_copy(inv_out.at[pl.ds(2 * i, 2)], p_raw, load_sem.at[0])
            pair.start()
            pair.wait()
            p_out[i, 0:BLOCK, 0:BLOCK] = p_raw[0].astype(jnp.bfloat16)
            p_out[i, BLOCK:TWIN, BLOCK:TWIN] = p_raw[1].astype(jnp.bfloat16)
            return carry

        lax.fori_loop(0, NBLK // 2, step, 0)

    gi_copy = remote(gi_send, gi_recv, gi_sem.at[0], gi_sem.at[1], sibling)

    def collect_x():
        def arrive(i, carry):
            for d in (2, 4, 6) + INDIRECT:
                xa_recv(i, d).wait_recv()

            @pl.when(jnp.logical_not(passing))
            def _():
                for d in DIRECT:
                    xa_recv(i, d).wait_recv()

            return carry

        lax.fori_loop(0, SHARE, arrive, 0)

        def turn_x(j, carry):
            cols = pl.ds(pl.multiple_of(j * tile, tile), tile)
            x_turned[cols, :] = x_all[:, cols].T
            return carry

        lax.fori_loop(0, HALF // tile, turn_x, 0)
        at = pl.ds(pl.multiple_of(quarter * TWIN, TWIN), TWIN)
        square[...] = mm(x_turned[at, :], x_all[:, at]) * (1.0 / TOKENS)
        for e in range(2):
            span = slice(e * BLOCK, (e + 1) * BLOCK)

            @pl.when(core == e)
            def _():
                gram_in[...] = square[span, span]

            @pl.when(core != e)
            def _():
                gi_send[...] = square[span, span]

        gi_copy.start()

    ahead = jnp.where(stage == last, 1, jnp.where(stage == last - 1, AHEAD, CHUNKS))

    def slot(t, carry):
        @pl.when(t < CHUNKS)
        def _():
            forward_own(t)
            forward_rest(t)
            forward_end(t)

        @pl.when((t == CHUNKS - 1) & hold_x)
        def _():
            def step(i, carry):
                for d in DIRECT:
                    xa_send(2 * i + core, d).start()
                return carry

            lax.fori_loop(0, SHARE, step, 0)

        @pl.when((t == CHUNKS - 1) & passing)
        def _():
            pass_all()

        @pl.when((t == CHUNKS - 1) & (2 * stage + CHUNKS <= 2 * last))
        def _():
            turn()

        @pl.when((t == CHUNKS - 1) & (stage == 0))
        def _():
            collect_x()

        @pl.when(t >= ahead - 1)
        def _():
            kb = t - (ahead - 1)
            backward_start(kb)
            backward_own(kb)
            backward_rest(kb)
            backward_end(kb)

        return carry

    @pl.when(2 * stage + CHUNKS > 2 * last)
    def _():
        turn()

    lax.fori_loop(0, CHUNKS + ahead - 1, slot, 0)

    @pl.when(hold_s)
    def _():
        def step(k, carry):
            @pl.when(lax.rem(k, 2) == core)
            def _():
                for d in range(1, CHIPS, 2):
                    sa_send(k, d).start()

            return carry

        lax.fori_loop(HELD, CHUNKS, step, 0)

    @pl.when(stage > 0)
    def _():
        collect_x()

    def arrive(i, carry):
        for d in range(1, CHIPS):
            sa_recv(i, d).wait_recv()
        return carry

    lax.fori_loop(0, SHARE, arrive, 0)

    def block(j, parity):
        rows = pl.ds(pl.multiple_of((2 * j + parity) * BLOCK, 16), BLOCK)
        return mm(x_turned[rows, :], s_all[...])

    def e_copy(n):
        return remote(e_send.at[n], e_recv.at[n], e_send_sem.at[n], e_recv_sem.at[n], sibling)

    def o_copy(n, j):
        owner = {"dp": (2 * upper + j // 2) * 4 + lax.rem(j, 2) * 2 + core}
        return remote(
            o_send.at[n], o_recv.at[quarter], o_send_sem.at[n], o_recv_sem.at[quarter], owner
        )

    def share(n, carry):
        e_send[n] = block(lax.rem(quarter + 1 + n, 4), 1 - core).astype(jnp.bfloat16)
        e_copy(n).start()
        return carry

    lax.fori_loop(0, 4, share, 0)

    def reduce(n, carry):
        j = lax.rem(quarter + 1 + n, 4)
        ours = block(j, core)
        e_copy(n).wait_recv()
        whole = (ours + e_recv[n].astype(jnp.float32)).astype(jnp.bfloat16)

        @pl.when(n < 3)
        def _():
            o_send[n] = whole
            o_copy(n, j).start()

        @pl.when(n == 3)
        def _():
            o_recv[quarter] = whole

        return carry

    lax.fori_loop(0, 4, reduce, 0)

    cols = pl.ds(pl.multiple_of(upper * TWIN, TWIN), TWIN)
    square[...] = gram(s_all[:, cols], s_all[:, cols]) * (1.0 / TOKENS)

    def go_remote(e, device):
        return remote(go_send.at[e], go_recv.at[core], go_send_sem.at[e], go_recv_sem.at[core], device)

    for e in range(2):
        span = slice(e * BLOCK, (e + 1) * BLOCK)
        go_send[e] = square[span, span]

        @pl.when(go_rank(e) == rank)
        def _():
            pltpu.make_async_copy(go_send.at[e], go_recv.at[core], go_recv_sem.at[core]).start()

        @pl.when(go_rank(e) != rank)
        def _():
            go_remote(e, {"dp": go_rank(e)}).start()

    def condition(n, carry):
        who = lax.rem(quarter + 4 - n, 4)

        @pl.when(n > 0)
        def _():
            here = o_recv.at[who]
            remote(here, here, o_send_sem.at[0], o_recv_sem.at[who], sibling).wait_recv()

        left = mm(p_in[...], o_recv[who]).astype(jnp.bfloat16)
        for j in range(2):
            right = mm(left[:, j * TWIN : (j + 1) * TWIN], p_out[2 * who + j])
            at = pl.ds(pl.multiple_of(who * QUAD + j * TWIN, TWIN), TWIN)
            update[:, at] = (right * (1.0 / TOKENS**0.5)).astype(jnp.bfloat16)
        return carry

    lax.fori_loop(0, 1, condition, 0)

    def drain(k, carry):
        for p in range(PIECES):

            @pl.when((stage < last) & (stage == 0))
            def _():
                f_copy(k, p).wait_send()

            @pl.when(stage > 0)
            def _():
                x_copy(k, p).wait_send()
                b_copy(k, p).wait_send()

            s_copy(k, p).wait_send()

        @pl.when((stage == 0) & (k // SHARE == core))
        def _():
            for h in range(2):
                i_copy(k, h).wait_send()

        @pl.when(lax.rem(k, 2) == core)
        def _():
            for d in range(1, CHIPS):
                sa_send(k, d).wait_send()
            for d in (2, 4, 6) + DIRECT:
                xa_send(k, d).wait_send()

            @pl.when(passing)
            def _():
                for d in DIRECT:
                    pass_on(k // 2, d).wait_send()

            @pl.when(jnp.logical_not(passing))
            def _():
                for d in INDIRECT:
                    xa_send(k, d).wait_send()


        return carry

    lax.fori_loop(0, CHUNKS, drain, 0)
    gi_copy.wait()
    gram_in[...] += gi_recv[...]
    for e in range(2):
        own = go_source(e) == rank

        @pl.when(own)
        def _():
            pltpu.make_async_copy(go_send.at[0], go_recv.at[e], go_recv_sem.at[e]).wait()

        @pl.when(jnp.logical_not(own))
        def _():
            here = go_recv.at[e]
            remote(here, here, go_send_sem.at[0], go_recv_sem.at[e], sibling).wait_recv()

    gram_out[...] = go_recv[0] + go_recv[1]

    lax.fori_loop(1, 4, condition, 0)

    for n in range(4):
        e_copy(n).wait_send()
    for n in range(3):
        o_copy(n, lax.rem(quarter + 1 + n, 4)).wait_send()
    for e in range(2):

        @pl.when(go_rank(e) != rank)
        def _():
            go_remote(e, sibling).wait_send()


def run_pipeline(counts, tokens, cotangent, matrix, inverse_in, inverse_out):
    dma = pltpu.SemaphoreType.DMA
    any_space = pl.BlockSpec(memory_space=pl.ANY)
    in_vmem = pl.BlockSpec(memory_space=pltpu.VMEM)
    pieces = (CHUNKS, PIECES)
    peers = (SHARE, CHIPS - 1)
    bf16, f32 = jnp.bfloat16, jnp.float32
    return pl.pallas_call(
        functools.partial(pipeline, lax.axis_size("section")),
        out_shape=[
            jax.ShapeDtypeStruct((BLOCK, D), bf16),
            jax.ShapeDtypeStruct((BLOCK, BLOCK), f32),
            jax.ShapeDtypeStruct((BLOCK, BLOCK), f32),
        ],
        in_specs=[pl.BlockSpec(memory_space=pltpu.SMEM)] + [any_space] * 5,
        out_specs=[in_vmem] * 3,
        scratch_shapes=[
            pltpu.VMEM((2, PAIR, HALF), bf16),
            pltpu.VMEM((2, PAIR, HALF), bf16),
            pltpu.VMEM((PAIR, HALF), bf16),
            pltpu.VMEM((PAIR, HALF), f32),
            pltpu.VMEM((PAIR, HALF), bf16),
            pltpu.VMEM((2, HALF, HALF), bf16),
            pltpu.VMEM((2, HALF, HALF), bf16),
            pltpu.VMEM((HALF, HALF), bf16),
            pltpu.VMEM((CHUNK, HALF), f32),
            pltpu.VMEM((SEEN, HALF), bf16),
            pltpu.VMEM((HALF, SEEN), bf16),
            pltpu.VMEM((SEEN, QUAD), bf16),
            pltpu.VMEM((4, BLOCK, QUAD), bf16),
            pltpu.VMEM((4, BLOCK, QUAD), bf16),
            pltpu.VMEM((3, BLOCK, QUAD), bf16),
            pltpu.VMEM((4, BLOCK, QUAD), bf16),
            pltpu.VMEM((2, BLOCK, BLOCK), f32),
            pltpu.VMEM((BLOCK, BLOCK), bf16),
            pltpu.VMEM((NBLK // 2, TWIN, TWIN), bf16),
            pltpu.VMEM((TWIN, TWIN), f32),
            pltpu.VMEM((BLOCK, BLOCK), f32),
            pltpu.VMEM((BLOCK, BLOCK), f32),
            pltpu.VMEM((2, BLOCK, BLOCK), f32),
            pltpu.VMEM((2, BLOCK, BLOCK), f32),
            dma((5,)),
            dma((1,)),
            dma((1,)),
        ]
        + [dma(pieces)] * 8
        + [dma(peers)] * 2
        + [dma((SHARE, 2))]
        + [dma(peers)] * 2
        + [dma((4,))] * 4
        + [dma((2,))] * 3,
        compiler_params=pltpu.CompilerParams(
            collective_id=0, has_side_effects=True, vmem_limit_bytes=62 * 2**20
        ),
        name="pipeline",
    )(counts, tokens, cotangent, matrix, inverse_in, inverse_out)


def shards(tokens, cotangent, live_counts, weight, inverse_in, inverse_out):
    update, owned_in, owned_out = run_pipeline(
        live_counts[0], tokens, cotangent, weight[0], inverse_in[0, 0], inverse_out[0]
    )
    return (update[None], owned_in[None, None], owned_out[None, None])


def solution(mesh):
    in_specs = (
        P("dp", None),
        P("dp", None),
        P("dp", None),
        P("section", None, None),
        P("section", "dp", None, None),
        P("section", None, None, None),
    )
    out_specs = (
        P("section", "dp", None),
        P("section", "dp", None, None),
        P("section", "dp", None, None),
    )
    return jax.shard_map(shards, mesh=mesh, in_specs=in_specs, out_specs=out_specs, check_vma=False)
```

```python
import functools

import jax
import jax.numpy as jnp
from jax import lax
from jax.experimental import pallas as pl
from jax.experimental.pallas import tpu as pltpu
from jax.sharding import PartitionSpec as P

D = 3072
HALF = D // 2
BLOCK = 192
MICRO = 4
ROWS = 80
TOK_DEV = 320
LIVE = 240
NBLK = 16
PAIR = 2 * LIVE
CHUNK = 48
CHUNKS = PAIR // CHUNK
PIECES = 2
WIDTH = HALF // PIECES

C_ZERO = 0.7978845608028654
C_ONE = 0.044715
MESH = pl.DeviceIdType.MESH
RING = 4
QUAD = 4 * BLOCK
TWIN = 2 * BLOCK
CHIPS = 8
SHARE = CHUNKS // 2
AHEAD = 6
HELD = 3
DIRECT = (1, 5)
INDIRECT = (3, 7)
SEEN = SHARE * CHIPS * CHUNK
TOKENS = 5120


def activate(value):
    return 0.5 * value * (1.0 + jnp.tanh(C_ZERO * (value + C_ONE * value * value * value)))


def slope(value):
    hyper = jnp.tanh(C_ZERO * (value + C_ONE * value * value * value))
    return 0.5 * (1.0 + hyper) + 0.5 * value * (1.0 - hyper * hyper) * C_ZERO * (
        1.0 + 3.0 * C_ONE * value * value
    )


def mm(a, b):
    return jnp.dot(a, b, preferred_element_type=jnp.float32)


def gram(a, b):
    return lax.dot_general(a, b, (((0,), (0,)), ((), ())), preferred_element_type=jnp.float32)


def pipeline(
    stages,
    counts,
    tokens,
    cotangent,
    weight,
    inv_in,
    inv_out,
    update,
    gram_in,
    gram_out,
    x_buf,
    s_buf,
    g_buf,
    slopes,
    h_send,
    w_fwd,
    w_bwd,
    w_raw,
    acc,
    x_all,
    x_turned,
    s_all,
    e_send,
    e_recv,
    o_recv,
    p_raw,
    p_in,
    p_out,
    square,
    gi_send,
    gi_recv,
    go_send,
    go_recv,
    load_sem,
    init_send,
    init_recv,
    f_send_sem,
    f_recv_sem,
    b_send_sem,
    b_recv_sem,
    xs_send_sem,
    xs_recv_sem,
    ss_send_sem,
    ss_recv_sem,
    xa_send_sem,
    xa_recv_sem,
    xp_send_sem,
    sa_send_sem,
    sa_recv_sem,
    e_send_sem,
    e_recv_sem,
    o_send_sem,
    o_recv_sem,
    gi_sem,
    go_send_sem,
    go_recv_sem,
):
    stage = lax.axis_index("section")
    rank = lax.axis_index("dp")
    core = lax.rem(rank, 2)
    side = lax.rem(rank // 2, 2)
    ring = rank // 4
    upper = ring // 2
    quarter = 2 * lax.rem(ring, 2) + side
    chip = rank // 2
    sibling = {"dp": rank + 1 - 2 * core}
    last = stages - 1
    following = {"section": jnp.minimum(stage + 1, last)}
    previous = {"section": jnp.maximum(stage - 1, 0)}
    own_cols = pl.ds(pl.multiple_of(core * HALF, HALF), HALF)
    sib_cols = pl.ds(pl.multiple_of((1 - core) * HALF, HALF), HALF)

    def chip_at(d):
        return 2 * lax.rem(ring + d // 2, RING) + lax.rem(side + d, 2)

    def chip_before(d):
        return 2 * lax.rem(ring + RING - d // 2, RING) + lax.rem(side + d, 2)

    def go_rank(e):
        return quarter * 4 + upper * 2 + e

    def go_source(e):
        return (2 * side + ring // 2) * 4 + lax.rem(ring, 2) * 2 + e

    def staged(which):
        return x_turned.at[pl.ds(pl.multiple_of(which * TOK_DEV, 16), TOK_DEV), pl.ds(0, HALF)]

    def fetch(array):
        return [
            pltpu.make_async_copy(
                array.at[:, pl.ds(h * HALF, HALF)], staged(h), load_sem.at[3 + h]
            )
            for h in range(2)
        ]

    loads = (
        pltpu.make_async_copy(weight.at[own_cols, own_cols], w_fwd.at[0], load_sem.at[0]),
        pltpu.make_async_copy(weight.at[sib_cols, own_cols], w_fwd.at[1], load_sem.at[1]),
        pltpu.make_async_copy(weight.at[own_cols, sib_cols], w_raw, load_sem.at[2]),
    )
    for load in loads[:2]:
        load.start()

    @pl.when(stage == 0)
    def _():
        for move in fetch(tokens):
            move.start()

    @pl.when(stage == last)
    def _():
        for move in fetch(cotangent):
            move.start()

    barrier = pltpu.get_barrier_semaphore()

    def greet(device):
        pl.semaphore_signal(barrier, inc=1, device_id=device, device_id_type=MESH)

    greet(sibling)
    for d in range(1, CHIPS):
        greet({"dp": 2 * chip_at(d) + core})

    @pl.when(stage > 0)
    def _():
        greet(previous)

    @pl.when(stage < last)
    def _():
        greet(following)

    for e in range(2):

        @pl.when(go_source(e) != rank)
        def _():
            greet({"dp": go_source(e)})

    expected = CHIPS + (stage > 0).astype(jnp.int32) + (stage < last).astype(jnp.int32)
    for e in range(2):
        expected = expected + (go_rank(e) != rank).astype(jnp.int32)
    pl.semaphore_wait(barrier, expected)

    def remote(src, dst, send, recv, device):
        return pltpu.make_async_remote_copy(
            src, dst, send, recv, device_id=device, device_id_type=MESH
        )

    def rows_of(k):
        return pl.ds(pl.multiple_of(k * CHUNK, 16), CHUNK)

    def i_copy(k, h):
        return remote(
            x_buf.at[h, rows_of(k)], x_buf.at[1 - h, rows_of(k)],
            xs_send_sem.at[k, h], xs_recv_sem.at[k, h], sibling,
        )

    mine = pl.ds(pl.multiple_of(core * LIVE, 16), LIVE)

    def chosen():
        slots = lax.broadcasted_iota(jnp.int32, (LIVE, TOK_DEV), 1)
        places = jnp.full((LIVE, TOK_DEV), -1, jnp.int32)
        begin = jnp.int32(0)
        for m in range(MICRO):
            count = counts[m]
            slot = slots - m * ROWS
            places = jnp.where((slot >= 0) & (slot < count), begin + slot, places)
            begin = begin + count
        return (places == lax.broadcasted_iota(jnp.int32, (LIVE, TOK_DEV), 0)).astype(jnp.bfloat16)

    def picked(pick, which):
        return mm(pick, staged(which)[...]).astype(jnp.bfloat16)

    @pl.when(stage == 0)
    def _():
        for move in fetch(tokens):
            move.wait()
        pick = chosen()
        x_buf[0, mine, :] = picked(pick, core)
        x_buf[1, mine, :] = picked(pick, 1 - core)

        def give(n, carry):
            for h in range(2):
                i_copy(core * SHARE + n, h).start()
            return carry

        lax.fori_loop(0, SHARE, give, 0)

    @pl.when(stage == last)
    def _():
        for move in fetch(cotangent):
            move.wait()
        pick = chosen()
        g_buf[mine, :] = picked(pick, core)
        h_send[mine, :] = picked(pick, 1 - core)
        give = remote(h_send.at[mine], g_buf.at[mine], init_send.at[0], init_recv.at[0], sibling)
        give.start()
        give.wait()

    for load in loads[:2]:
        load.wait()
    loads[2].start()

    def cols_of(p):
        return pl.ds(p * WIDTH, WIDTH)

    def f_copy(k, p):
        at = (rows_of(k), cols_of(p))
        return remote(
            h_send.at[at], x_buf.at[(0,) + at], f_send_sem.at[k, p], f_recv_sem.at[k, p], following
        )

    def b_copy(k, p):
        at = (rows_of(k), cols_of(p))
        return remote(
            h_send.at[at], g_buf.at[at], b_send_sem.at[k, p], b_recv_sem.at[k, p], previous
        )

    def x_copy(k, p):
        at = (rows_of(k), cols_of(p))
        return remote(
            x_buf.at[(0,) + at], x_buf.at[(1,) + at], xs_send_sem.at[k, p], xs_recv_sem.at[k, p],
            sibling,
        )

    def s_copy(k, p):
        at = (rows_of(k), cols_of(p))
        return remote(
            s_buf.at[(0,) + at], s_buf.at[(1,) + at], ss_send_sem.at[k, p], ss_recv_sem.at[k, p],
            sibling,
        )

    hold_x = stage == last // 2
    hold_s = stage == last // 2 + 1
    passing = hold_x | hold_s

    def x_part(to, k):
        which = jnp.where(to // 4 == core, 0, 1)
        return x_buf.at[which, rows_of(k)]

    def s_part(to, k):
        which = jnp.where(lax.rem(to // 2, 2) == core, 0, 1)
        cols = pl.ds(pl.multiple_of(lax.rem(to, 2) * QUAD, QUAD), QUAD)
        return s_buf.at[which, rows_of(k), cols]

    def slot_of(i, who):
        return pl.ds(pl.multiple_of((i * CHIPS + who) * CHUNK, 16), CHUNK)

    def xa_send(k, d):
        i = k // 2
        return remote(
            x_part(chip_at(d), k), x_all.at[slot_of(i, chip)],
            xa_send_sem.at[i, d - 1], xa_recv_sem.at[i, d - 1], {"dp": 2 * chip_at(d) + core},
        )

    def xa_recv(i, d):
        here = x_all.at[slot_of(i, chip_before(d))]
        return remote(here, here, xa_send_sem.at[i, d - 1], xa_recv_sem.at[i, d - 1], sibling)

    def pass_on(i, d):
        here = x_all.at[slot_of(i, chip_before(d))]
        beside = ring + 1 - 2 * lax.rem(ring, 2)
        away = lax.rem(beside - ring + d // 2 + RING, RING)
        return remote(
            here, here, xp_send_sem.at[i, d // 4], xa_recv_sem.at[i, 2 * away],
            {"dp": 4 * beside + lax.rem(rank, 4)},
        )

    def pass_all():
        def step(i, carry):
            for d in DIRECT:
                xa_recv(i, d).wait_recv()
                pass_on(i, d).start()
            return carry

        lax.fori_loop(0, SHARE, step, 0)

    def sa_send(k, d):
        i = k // 2
        return remote(
            s_part(chip_at(d), k), s_all.at[slot_of(i, chip)],
            sa_send_sem.at[i, d - 1], sa_recv_sem.at[i, d - 1], {"dp": 2 * chip_at(d) + core},
        )

    def sa_recv(i, d):
        here = s_all.at[slot_of(i, chip_before(d))]
        return remote(here, here, sa_send_sem.at[i, d - 1], sa_recv_sem.at[i, d - 1], sibling)

    end = cols_of(PIECES - 1)

    def wide_rows(k, span):
        return pl.ds(pl.multiple_of(k * CHUNK, 16), span * CHUNK)

    def forward_own(k, span):
        rows, some = wide_rows(k, span), pl.ds(0, span * CHUNK)

        @pl.when((stage == 0) & (k // SHARE != core))
        def _():
            for h in range(2):
                i_copy(k, h).wait_recv()

        for p in range(PIECES):
            cols = cols_of(p)

            @pl.when(stage > 0)
            def _():
                for q in range(span):
                    f_copy(k + q, p).wait_recv()
                    x_copy(k + q, p).start()

            term = mm(x_buf[0, rows, cols], w_fwd[0, cols, :])
            acc[some, :] = term if p == 0 else acc[some, :] + term

    def forward_rest(k, span):
        rows, some = wide_rows(k, span), pl.ds(0, span * CHUNK)
        for p in range(PIECES):

            @pl.when(stage > 0)
            def _():
                for q in range(span):
                    x_copy(k + q, p).wait_recv()

            cols = cols_of(p)
            if p < PIECES - 1:
                acc[some, :] += mm(x_buf[1, rows, cols], w_fwd[1, cols, :])
        for p in range(PIECES):
            cols = cols_of(p)
            pre = acc[some, cols] + mm(x_buf[1, rows, end], w_fwd[1, end, cols])
            acc[some, cols] = pre
            if span == 1:

                @pl.when(stage < last)
                def _():
                    h_send[rows, cols] = (
                        x_buf[0, rows, cols].astype(jnp.float32) + activate(pre)
                    ).astype(jnp.bfloat16)
                    f_copy(k, p).start()

    def forward_end(k, span):
        rows = wide_rows(k, span)
        slopes[rows, :] = slope(acc[pl.ds(0, span * CHUNK), :]).astype(jnp.bfloat16)
        for q in range(span):

            @pl.when(lax.rem(k + q, 2) == core)
            def _():
                for d in range(2, CHIPS, 2):
                    xa_send(k + q, d).start()

                @pl.when(jnp.logical_not(hold_x))
                def _():
                    for d in DIRECT:
                        xa_send(k + q, d).start()

                @pl.when(jnp.logical_not(passing))
                def _():
                    for d in INDIRECT:
                        xa_send(k + q, d).start()

                which = jnp.where(upper == core, 0, 1)
                x_all[slot_of((k + q) // 2, chip), :] = x_buf[which, rows_of(k + q), :]

    def backward_start(k, span):
        rows = wide_rows(k, span)
        for p in range(PIECES):
            cols = cols_of(p)

            if span == 1:

                @pl.when(stage < last)
                def _():
                    b_copy(k, p).wait_recv()

            s_buf[0, rows, cols] = (
                g_buf[rows, cols].astype(jnp.float32) * slopes[rows, cols].astype(jnp.float32)
            ).astype(jnp.bfloat16)
            for q in range(span):
                s_copy(k + q, p).start()

    def backward_own(k, span):
        @pl.when(stage > 0)
        def _():
            acc[pl.ds(0, span * CHUNK), :] = mm(s_buf[0, wide_rows(k, span), :], w_bwd[0])

    def backward_rest(k, span):
        rows, some = wide_rows(k, span), pl.ds(0, span * CHUNK)
        for p in range(PIECES):
            for q in range(span):
                s_copy(k + q, p).wait_recv()
            cols = cols_of(p)
            if p < PIECES - 1:

                @pl.when(stage > 0)
                def _():
                    acc[some, :] += mm(s_buf[1, rows, cols], w_bwd[1, cols, :])

        @pl.when(stage > 0)
        def _():
            if span == 1:

                @pl.when(stage < last)
                def _():
                    for p in range(PIECES):
                        f_copy(k, p).wait_send()

            for p in range(PIECES):
                cols = cols_of(p)
                back = acc[some, cols] + mm(s_buf[1, rows, end], w_bwd[1, end, cols])
                h_send[rows, cols] = (
                    g_buf[rows, cols].astype(jnp.float32) + back
                ).astype(jnp.bfloat16)
                b_copy(k, p).start()
            for q in range(1, span):
                for p in range(PIECES):
                    b_copy(k + q, p).start()

    def backward_end(k, span):
        for q in range(span):

            @pl.when(lax.rem(k + q, 2) == core)
            def _():
                for d in range(2, CHIPS, 2):
                    sa_send(k + q, d).start()

                @pl.when(jnp.logical_not(hold_s) | (k + q < HELD))
                def _():
                    for d in range(1, CHIPS, 2):
                        sa_send(k + q, d).start()

                which = jnp.where(lax.rem(ring, 2) == core, 0, 1)
                cols = pl.ds(pl.multiple_of(side * QUAD, QUAD), QUAD)
                s_all[slot_of((k + q) // 2, chip), :] = s_buf[which, rows_of(k + q), cols]

    def forward(k, span):
        forward_own(k, span)
        forward_rest(k, span)
        forward_end(k, span)

    def backward(k, span):
        backward_start(k, span)
        backward_own(k, span)
        backward_rest(k, span)
        backward_end(k, span)

    tile = 256

    def turn():
        loads[2].wait()

        @pl.when(stage > 0)
        def _():
            def step(i, carry):
                at = pl.ds(pl.multiple_of(i * tile, tile), tile)
                for j in range(HALF // tile):
                    to = pl.ds(j * tile, tile)
                    w_bwd[0, to, at] = w_fwd[0, at, to].T
                    w_bwd[1, to, at] = w_raw[at, to].T
                return carry

            lax.fori_loop(0, HALF // tile, step, 0)

        load = pltpu.make_async_copy(inv_in, p_raw.at[0], load_sem.at[0])
        load.start()
        load.wait()
        p_in[...] = p_raw[0].astype(jnp.bfloat16)
        p_out[...] = jnp.zeros_like(p_out)

        def step(i, carry):
            pair = pltpu.make_async_copy(inv_out.at[pl.ds(2 * i, 2)], p_raw, load_sem.at[0])
            pair.start()
            pair.wait()
            p_out[i, 0:BLOCK, 0:BLOCK] = p_raw[0].astype(jnp.bfloat16)
            p_out[i, BLOCK:TWIN, BLOCK:TWIN] = p_raw[1].astype(jnp.bfloat16)
            return carry

        lax.fori_loop(0, NBLK // 2, step, 0)

    gi_copy = remote(gi_send, gi_recv, gi_sem.at[0], gi_sem.at[1], sibling)

    def collect_x():
        def arrive(i, carry):
            for d in (2, 4, 6) + INDIRECT:
                xa_recv(i, d).wait_recv()

            @pl.when(jnp.logical_not(passing))
            def _():
                for d in DIRECT:
                    xa_recv(i, d).wait_recv()

            return carry

        lax.fori_loop(0, SHARE, arrive, 0)

        def turn_x(j, carry):
            cols = pl.ds(pl.multiple_of(j * tile, tile), tile)
            x_turned[cols, :] = x_all[:, cols].T
            return carry

        lax.fori_loop(0, HALF // tile, turn_x, 0)
        at = pl.ds(pl.multiple_of(quarter * TWIN, TWIN), TWIN)
        square[...] = mm(x_turned[at, :], x_all[:, at]) * (1.0 / TOKENS)
        for e in range(2):
            span = slice(e * BLOCK, (e + 1) * BLOCK)

            @pl.when(core == e)
            def _():
                gram_in[...] = square[span, span]

            @pl.when(core != e)
            def _():
                gi_send[...] = square[span, span]

        gi_copy.start()

    ahead = jnp.where(stage == last, 1, jnp.where(stage == last - 1, AHEAD, CHUNKS))

    def slot(t, carry):
        kf = jnp.where(stage == last, jnp.where(t == 0, 0, CHUNKS - 1), t)
        kb = jnp.where(stage == last, kf, t - (ahead - 1))
        alone = (stage < last) | (t == 0) | (t == CHUNKS // 2)

        @pl.when(alone & (kf < CHUNKS))
        def _():
            forward(kf, 1)

        @pl.when((t == CHUNKS - 1) & hold_x)
        def _():
            def step(i, carry):
                for d in DIRECT:
                    xa_send(2 * i + core, d).start()
                return carry

            lax.fori_loop(0, SHARE, step, 0)

        @pl.when((t == CHUNKS - 1) & passing)
        def _():
            pass_all()

        @pl.when((t == CHUNKS - 1) & (2 * stage + CHUNKS <= 2 * last))
        def _():
            turn()

        @pl.when((t == CHUNKS - 1) & (stage == 0))
        def _():
            collect_x()

        @pl.when(alone & (kb >= 0))
        def _():
            backward(kb, 1)

        @pl.when(jnp.logical_not(alone))
        def _():
            forward(2 * t - 1, 2)
            backward(2 * t - 1, 2)

        return carry

    @pl.when(2 * stage + CHUNKS > 2 * last)
    def _():
        turn()

    lax.fori_loop(0, jnp.where(stage == last, CHUNKS // 2 + 1, CHUNKS + ahead - 1), slot, 0)

    @pl.when(hold_s)
    def _():
        def step(k, carry):
            @pl.when(lax.rem(k, 2) == core)
            def _():
                for d in range(1, CHIPS, 2):
                    sa_send(k, d).start()

            return carry

        lax.fori_loop(HELD, CHUNKS, step, 0)

    @pl.when(stage > 0)
    def _():
        collect_x()

    def arrive(i, carry):
        for d in range(1, CHIPS):
            sa_recv(i, d).wait_recv()
        return carry

    lax.fori_loop(0, SHARE, arrive, 0)

    def block(j, parity):
        rows = pl.ds(pl.multiple_of((2 * j + parity) * BLOCK, 16), BLOCK)
        return mm(x_turned[rows, :], s_all[...])

    def e_copy(n):
        return remote(e_send.at[n], e_recv.at[n], e_send_sem.at[n], e_recv_sem.at[n], sibling)

    def o_copy(n, j):
        owner = {"dp": (2 * upper + j // 2) * 4 + lax.rem(j, 2) * 2 + core}
        return remote(
            e_send.at[n], o_recv.at[quarter], o_send_sem.at[n], o_recv_sem.at[quarter], owner
        )

    def share(n, carry):
        e_send[n] = block(lax.rem(quarter + 1 + n, 4), 1 - core).astype(jnp.bfloat16)
        e_copy(n).start()
        return carry

    lax.fori_loop(0, 4, share, 0)

    def reduce(n, carry):
        j = lax.rem(quarter + 1 + n, 4)
        ours = block(j, core)
        e_copy(n).wait_recv()
        whole = (ours + e_recv[n].astype(jnp.float32)).astype(jnp.bfloat16)

        @pl.when(n < 3)
        def _():
            e_copy(n).wait_send()
            e_send[n] = whole
            o_copy(n, j).start()

        @pl.when(n == 3)
        def _():
            o_recv[quarter] = whole

        return carry

    lax.fori_loop(0, 4, reduce, 0)

    cols = pl.ds(pl.multiple_of(upper * TWIN, TWIN), TWIN)
    square[...] = gram(s_all[:, cols], s_all[:, cols]) * (1.0 / TOKENS)

    def go_remote(e, device):
        return remote(go_send.at[e], go_recv.at[core], go_send_sem.at[e], go_recv_sem.at[core], device)

    for e in range(2):
        span = slice(e * BLOCK, (e + 1) * BLOCK)
        go_send[e] = square[span, span]

        @pl.when(go_rank(e) == rank)
        def _():
            pltpu.make_async_copy(go_send.at[e], go_recv.at[core], go_recv_sem.at[core]).start()

        @pl.when(go_rank(e) != rank)
        def _():
            go_remote(e, {"dp": go_rank(e)}).start()

    def condition(n, carry):
        who = lax.rem(quarter + 4 - n, 4)

        @pl.when(n > 0)
        def _():
            here = o_recv.at[who]
            remote(here, here, o_send_sem.at[0], o_recv_sem.at[who], sibling).wait_recv()

        left = mm(p_in[...], o_recv[who]).astype(jnp.bfloat16)
        for j in range(2):
            right = mm(left[:, j * TWIN : (j + 1) * TWIN], p_out[2 * who + j])
            at = pl.ds(pl.multiple_of(who * QUAD + j * TWIN, TWIN), TWIN)
            update[:, at] = (right * (1.0 / TOKENS**0.5)).astype(jnp.bfloat16)
        return carry

    lax.fori_loop(0, 1, condition, 0)

    def drain(k, carry):
        for p in range(PIECES):

            @pl.when((stage < last) & (stage == 0))
            def _():
                f_copy(k, p).wait_send()

            @pl.when(stage > 0)
            def _():
                x_copy(k, p).wait_send()
                b_copy(k, p).wait_send()

            s_copy(k, p).wait_send()

        @pl.when((stage == 0) & (k // SHARE == core))
        def _():
            for h in range(2):
                i_copy(k, h).wait_send()

        @pl.when(lax.rem(k, 2) == core)
        def _():
            for d in range(1, CHIPS):
                sa_send(k, d).wait_send()
            for d in (2, 4, 6) + DIRECT:
                xa_send(k, d).wait_send()

            @pl.when(passing)
            def _():
                for d in DIRECT:
                    pass_on(k // 2, d).wait_send()

            @pl.when(jnp.logical_not(passing))
            def _():
                for d in INDIRECT:
                    xa_send(k, d).wait_send()


        return carry

    lax.fori_loop(0, CHUNKS, drain, 0)
    gi_copy.wait()
    gram_in[...] += gi_recv[...]
    for e in range(2):
        own = go_source(e) == rank

        @pl.when(own)
        def _():
            pltpu.make_async_copy(go_send.at[0], go_recv.at[e], go_recv_sem.at[e]).wait()

        @pl.when(jnp.logical_not(own))
        def _():
            here = go_recv.at[e]
            remote(here, here, go_send_sem.at[0], go_recv_sem.at[e], sibling).wait_recv()

    gram_out[...] = go_recv[0] + go_recv[1]

    lax.fori_loop(1, 4, condition, 0)

    e_copy(3).wait_send()
    for n in range(3):
        o_copy(n, lax.rem(quarter + 1 + n, 4)).wait_send()
    for e in range(2):

        @pl.when(go_rank(e) != rank)
        def _():
            go_remote(e, sibling).wait_send()


def run_pipeline(counts, tokens, cotangent, matrix, inverse_in, inverse_out):
    dma = pltpu.SemaphoreType.DMA
    any_space = pl.BlockSpec(memory_space=pl.ANY)
    in_vmem = pl.BlockSpec(memory_space=pltpu.VMEM)
    pieces = (CHUNKS, PIECES)
    peers = (SHARE, CHIPS - 1)
    bf16, f32 = jnp.bfloat16, jnp.float32
    return pl.pallas_call(
        functools.partial(pipeline, lax.axis_size("section")),
        out_shape=[
            jax.ShapeDtypeStruct((BLOCK, D), bf16),
            jax.ShapeDtypeStruct((BLOCK, BLOCK), f32),
            jax.ShapeDtypeStruct((BLOCK, BLOCK), f32),
        ],
        in_specs=[pl.BlockSpec(memory_space=pltpu.SMEM)] + [any_space] * 5,
        out_specs=[in_vmem] * 3,
        scratch_shapes=[
            pltpu.VMEM((2, PAIR, HALF), bf16),
            pltpu.VMEM((2, PAIR, HALF), bf16),
            pltpu.VMEM((PAIR, HALF), bf16),
            pltpu.VMEM((PAIR, HALF), bf16),
            pltpu.VMEM((PAIR, HALF), bf16),
            pltpu.VMEM((2, HALF, HALF), bf16),
            pltpu.VMEM((2, HALF, HALF), bf16),
            pltpu.VMEM((HALF, HALF), bf16),
            pltpu.VMEM((2 * CHUNK, HALF), f32),
            pltpu.VMEM((SEEN, HALF), bf16),
            pltpu.VMEM((HALF, SEEN), bf16),
            pltpu.VMEM((SEEN, QUAD), bf16),
            pltpu.VMEM((4, BLOCK, QUAD), bf16),
            pltpu.VMEM((4, BLOCK, QUAD), bf16),
            pltpu.VMEM((4, BLOCK, QUAD), bf16),
            pltpu.VMEM((2, BLOCK, BLOCK), f32),
            pltpu.VMEM((BLOCK, BLOCK), bf16),
            pltpu.VMEM((NBLK // 2, TWIN, TWIN), bf16),
            pltpu.VMEM((TWIN, TWIN), f32),
            pltpu.VMEM((BLOCK, BLOCK), f32),
            pltpu.VMEM((BLOCK, BLOCK), f32),
            pltpu.VMEM((2, BLOCK, BLOCK), f32),
            pltpu.VMEM((2, BLOCK, BLOCK), f32),
            dma((5,)),
            dma((1,)),
            dma((1,)),
        ]
        + [dma(pieces)] * 8
        + [dma(peers)] * 2
        + [dma((SHARE, 2))]
        + [dma(peers)] * 2
        + [dma((4,))] * 4
        + [dma((2,))] * 3,
        compiler_params=pltpu.CompilerParams(
            collective_id=0, has_side_effects=True, vmem_limit_bytes=62 * 2**20
        ),
        name="pipeline",
    )(counts, tokens, cotangent, matrix, inverse_in, inverse_out)


def hand_over(*refs):
    for i in range(3):
        refs[3 + i][...] = refs[i][...]


def outputs(*arrays):
    in_vmem = pl.BlockSpec(memory_space=pltpu.VMEM)
    return pl.pallas_call(
        hand_over,
        out_shape=[jax.ShapeDtypeStruct(a.shape, a.dtype) for a in arrays],
        in_specs=[in_vmem] * 3,
        out_specs=[in_vmem] * 3,
        name="outputs",
    )(*arrays)


def shards(tokens, cotangent, live_counts, weight, inverse_in, inverse_out):
    results = run_pipeline(
        live_counts[0], tokens, cotangent, weight[0], inverse_in[0, 0], inverse_out[0]
    )
    update, owned_in, owned_out = outputs(*results)
    return (update[None], owned_in[None, None], owned_out[None, None])


def solution(mesh):
    in_specs = (
        P("dp", None),
        P("dp", None),
        P("dp", None),
        P("section", None, None),
        P("section", "dp", None, None),
        P("section", None, None, None),
    )
    out_specs = (
        P("section", "dp", None),
        P("section", "dp", None, None),
        P("section", "dp", None, None),
    )
    return jax.shard_map(shards, mesh=mesh, in_specs=in_specs, out_specs=out_specs, check_vma=False)
```

```python
import functools

import jax
import jax.numpy as jnp
from jax import lax
from jax.experimental import pallas as pl
from jax.experimental.pallas import tpu as pltpu
from jax.sharding import PartitionSpec as P

D = 3072
HALF = D // 2
BLOCK = 192
MICRO = 4
ROWS = 80
TOK_DEV = 320
LIVE = 240
NBLK = 16
PAIR = 2 * LIVE
CHUNK = 48
CHUNKS = PAIR // CHUNK
PIECES = 2
WIDTH = HALF // PIECES

C_ZERO = 0.7978845608028654
C_ONE = 0.044715
MESH = pl.DeviceIdType.MESH
RING = 4
QUAD = 4 * BLOCK
TWIN = 2 * BLOCK
CHIPS = 8
SHARE = CHUNKS // 2
AHEAD = 6
HELD = 3
DIRECT = (1, 5)
INDIRECT = (3, 7)
SEEN = SHARE * CHIPS * CHUNK
TOKENS = 5120


def activate(value):
    return 0.5 * value * (1.0 + jnp.tanh(C_ZERO * (value + C_ONE * value * value * value)))


def slope(value):
    hyper = jnp.tanh(C_ZERO * (value + C_ONE * value * value * value))
    return 0.5 * (1.0 + hyper) + 0.5 * value * (1.0 - hyper * hyper) * C_ZERO * (
        1.0 + 3.0 * C_ONE * value * value
    )


def mm(a, b):
    return jnp.dot(a, b, preferred_element_type=jnp.float32)


def gram(a, b):
    return lax.dot_general(a, b, (((0,), (0,)), ((), ())), preferred_element_type=jnp.float32)


def pipeline(
    stages,
    counts,
    tokens,
    cotangent,
    weight,
    inv_in,
    inv_out,
    update,
    gram_in,
    gram_out,
    x_buf,
    s_buf,
    g_buf,
    slopes,
    h_send,
    w_fwd,
    w_bwd,
    w_raw,
    acc,
    x_all,
    x_turned,
    s_all,
    e_send,
    e_recv,
    o_recv,
    p_raw,
    p_in,
    p_out,
    square,
    gi_send,
    gi_recv,
    go_send,
    go_recv,
    load_sem,
    init_send,
    init_recv,
    f_send_sem,
    f_recv_sem,
    b_send_sem,
    b_recv_sem,
    xs_send_sem,
    xs_recv_sem,
    ss_send_sem,
    ss_recv_sem,
    xa_send_sem,
    xa_recv_sem,
    xp_send_sem,
    sa_send_sem,
    sa_recv_sem,
    e_send_sem,
    e_recv_sem,
    o_send_sem,
    o_recv_sem,
    gi_sem,
    go_send_sem,
    go_recv_sem,
):
    stage = lax.axis_index("section")
    rank = lax.axis_index("dp")
    core = lax.rem(rank, 2)
    side = lax.rem(rank // 2, 2)
    ring = rank // 4
    upper = ring // 2
    quarter = 2 * lax.rem(ring, 2) + side
    chip = rank // 2
    sibling = {"dp": rank + 1 - 2 * core}
    last = stages - 1
    following = {"section": jnp.minimum(stage + 1, last)}
    previous = {"section": jnp.maximum(stage - 1, 0)}
    own_cols = pl.ds(pl.multiple_of(core * HALF, HALF), HALF)
    sib_cols = pl.ds(pl.multiple_of((1 - core) * HALF, HALF), HALF)

    def chip_at(d):
        return 2 * lax.rem(ring + d // 2, RING) + lax.rem(side + d, 2)

    def chip_before(d):
        return 2 * lax.rem(ring + RING - d // 2, RING) + lax.rem(side + d, 2)

    def go_rank(e):
        return quarter * 4 + upper * 2 + e

    def go_source(e):
        return (2 * side + ring // 2) * 4 + lax.rem(ring, 2) * 2 + e

    def staged(which):
        return x_turned.at[pl.ds(pl.multiple_of(which * TOK_DEV, 16), TOK_DEV), pl.ds(0, HALF)]

    def fetch(array):
        return [
            pltpu.make_async_copy(
                array.at[:, pl.ds(h * HALF, HALF)], staged(h), load_sem.at[3 + h]
            )
            for h in range(2)
        ]

    loads = (
        pltpu.make_async_copy(weight.at[own_cols, own_cols], w_fwd.at[0], load_sem.at[0]),
        pltpu.make_async_copy(weight.at[sib_cols, own_cols], w_fwd.at[1], load_sem.at[1]),
        pltpu.make_async_copy(weight.at[own_cols, sib_cols], w_raw, load_sem.at[2]),
    )
    @pl.when(stage == 0)
    def _():
        for move in fetch(tokens):
            move.start()

    @pl.when(stage == last)
    def _():
        for move in fetch(cotangent):
            move.start()

    for load in loads[:2]:
        load.start()

    barrier = pltpu.get_barrier_semaphore()

    def greet(device):
        pl.semaphore_signal(barrier, inc=1, device_id=device, device_id_type=MESH)

    greet(sibling)
    for d in range(1, CHIPS):
        greet({"dp": 2 * chip_at(d) + core})

    @pl.when(stage > 0)
    def _():
        greet(previous)

    @pl.when(stage < last)
    def _():
        greet(following)

    for e in range(2):

        @pl.when(go_source(e) != rank)
        def _():
            greet({"dp": go_source(e)})

    expected = CHIPS + (stage > 0).astype(jnp.int32) + (stage < last).astype(jnp.int32)
    for e in range(2):
        expected = expected + (go_rank(e) != rank).astype(jnp.int32)
    pl.semaphore_wait(barrier, expected)

    def remote(src, dst, send, recv, device):
        return pltpu.make_async_remote_copy(
            src, dst, send, recv, device_id=device, device_id_type=MESH
        )

    def rows_of(k):
        return pl.ds(pl.multiple_of(k * CHUNK, 16), CHUNK)

    def i_copy(k, h):
        return remote(
            x_buf.at[h, rows_of(k)], x_buf.at[1 - h, rows_of(k)],
            xs_send_sem.at[k, h], xs_recv_sem.at[k, h], sibling,
        )

    mine = pl.ds(pl.multiple_of(core * LIVE, 16), LIVE)

    def chosen():
        slots = lax.broadcasted_iota(jnp.int32, (LIVE, TOK_DEV), 1)
        places = jnp.full((LIVE, TOK_DEV), -1, jnp.int32)
        begin = jnp.int32(0)
        for m in range(MICRO):
            count = counts[m]
            slot = slots - m * ROWS
            places = jnp.where((slot >= 0) & (slot < count), begin + slot, places)
            begin = begin + count
        return (places == lax.broadcasted_iota(jnp.int32, (LIVE, TOK_DEV), 0)).astype(jnp.bfloat16)

    def picked(pick, which):
        return mm(pick, staged(which)[...]).astype(jnp.bfloat16)

    @pl.when(stage == 0)
    def _():
        for move in fetch(tokens):
            move.wait()
        pick = chosen()
        x_buf[0, mine, :] = picked(pick, core)
        x_buf[1, mine, :] = picked(pick, 1 - core)

        def give(n, carry):
            for h in range(2):
                i_copy(core * SHARE + n, h).start()
            return carry

        lax.fori_loop(0, SHARE, give, 0)

    @pl.when(stage == last)
    def _():
        for move in fetch(cotangent):
            move.wait()
        pick = chosen()
        g_buf[mine, :] = picked(pick, core)
        h_send[mine, :] = picked(pick, 1 - core)
        give = remote(h_send.at[mine], g_buf.at[mine], init_send.at[0], init_recv.at[0], sibling)
        give.start()
        give.wait()

    for load in loads[:2]:
        load.wait()
    loads[2].start()

    def cols_of(p):
        return pl.ds(p * WIDTH, WIDTH)

    def f_copy(k, p):
        at = (rows_of(k), cols_of(p))
        return remote(
            h_send.at[at], x_buf.at[(0,) + at], f_send_sem.at[k, p], f_recv_sem.at[k, p], following
        )

    def b_copy(k, p):
        at = (rows_of(k), cols_of(p))
        return remote(
            h_send.at[at], g_buf.at[at], b_send_sem.at[k, p], b_recv_sem.at[k, p], previous
        )

    def x_copy(k, p):
        at = (rows_of(k), cols_of(p))
        return remote(
            x_buf.at[(0,) + at], x_buf.at[(1,) + at], xs_send_sem.at[k, p], xs_recv_sem.at[k, p],
            sibling,
        )

    def s_copy(k, p):
        at = (rows_of(k), cols_of(p))
        return remote(
            s_buf.at[(0,) + at], s_buf.at[(1,) + at], ss_send_sem.at[k, p], ss_recv_sem.at[k, p],
            sibling,
        )

    hold_x = stage == last // 2
    hold_s = stage == last // 2 + 1
    passing = hold_x | hold_s

    def x_part(to, k):
        which = jnp.where(to // 4 == core, 0, 1)
        return x_buf.at[which, rows_of(k)]

    def s_part(to, k):
        which = jnp.where(lax.rem(to // 2, 2) == core, 0, 1)
        cols = pl.ds(pl.multiple_of(lax.rem(to, 2) * QUAD, QUAD), QUAD)
        return s_buf.at[which, rows_of(k), cols]

    def slot_of(i, who):
        return pl.ds(pl.multiple_of((i * CHIPS + who) * CHUNK, 16), CHUNK)

    def xa_send(k, d):
        i = k // 2
        return remote(
            x_part(chip_at(d), k), x_all.at[slot_of(i, chip)],
            xa_send_sem.at[i, d - 1], xa_recv_sem.at[i, d - 1], {"dp": 2 * chip_at(d) + core},
        )

    def xa_recv(i, d):
        here = x_all.at[slot_of(i, chip_before(d))]
        return remote(here, here, xa_send_sem.at[i, d - 1], xa_recv_sem.at[i, d - 1], sibling)

    def pass_on(i, d):
        here = x_all.at[slot_of(i, chip_before(d))]
        beside = ring + 1 - 2 * lax.rem(ring, 2)
        away = lax.rem(beside - ring + d // 2 + RING, RING)
        return remote(
            here, here, xp_send_sem.at[i, d // 4], xa_recv_sem.at[i, 2 * away],
            {"dp": 4 * beside + lax.rem(rank, 4)},
        )

    def pass_all():
        def step(i, carry):
            for d in DIRECT:
                xa_recv(i, d).wait_recv()
                pass_on(i, d).start()
            return carry

        lax.fori_loop(0, SHARE, step, 0)

    def sa_send(k, d):
        i = k // 2
        return remote(
            s_part(chip_at(d), k), s_all.at[slot_of(i, chip)],
            sa_send_sem.at[i, d - 1], sa_recv_sem.at[i, d - 1], {"dp": 2 * chip_at(d) + core},
        )

    def sa_recv(i, d):
        here = s_all.at[slot_of(i, chip_before(d))]
        return remote(here, here, sa_send_sem.at[i, d - 1], sa_recv_sem.at[i, d - 1], sibling)

    end = cols_of(PIECES - 1)

    def wide_rows(k, span):
        return pl.ds(pl.multiple_of(k * CHUNK, 16), span * CHUNK)

    def forward_own(k, span):
        rows, some = wide_rows(k, span), pl.ds(0, span * CHUNK)

        @pl.when((stage == 0) & (k // SHARE != core))
        def _():
            for h in range(2):
                i_copy(k, h).wait_recv()

        for p in range(PIECES):
            cols = cols_of(p)

            @pl.when(stage > 0)
            def _():
                for q in range(span):
                    f_copy(k + q, p).wait_recv()
                    x_copy(k + q, p).start()

            term = mm(x_buf[0, rows, cols], w_fwd[0, cols, :])
            acc[some, :] = term if p == 0 else acc[some, :] + term

    def forward_rest(k, span):
        rows, some = wide_rows(k, span), pl.ds(0, span * CHUNK)
        for p in range(PIECES):

            @pl.when(stage > 0)
            def _():
                for q in range(span):
                    x_copy(k + q, p).wait_recv()

            cols = cols_of(p)
            if p < PIECES - 1:
                acc[some, :] += mm(x_buf[1, rows, cols], w_fwd[1, cols, :])
        for p in range(PIECES):
            cols = cols_of(p)
            pre = acc[some, cols] + mm(x_buf[1, rows, end], w_fwd[1, end, cols])
            acc[some, cols] = pre
            if span == 1:

                @pl.when(stage < last)
                def _():
                    h_send[rows, cols] = (
                        x_buf[0, rows, cols].astype(jnp.float32) + activate(pre)
                    ).astype(jnp.bfloat16)
                    f_copy(k, p).start()

    def forward_end(k, span):
        rows = wide_rows(k, span)
        slopes[rows, :] = slope(acc[pl.ds(0, span * CHUNK), :]).astype(jnp.bfloat16)
        for q in range(span):

            @pl.when(lax.rem(k + q, 2) == core)
            def _():
                for d in range(2, CHIPS, 2):
                    xa_send(k + q, d).start()

                @pl.when(jnp.logical_not(hold_x))
                def _():
                    for d in DIRECT:
                        xa_send(k + q, d).start()

                @pl.when(jnp.logical_not(passing))
                def _():
                    for d in INDIRECT:
                        xa_send(k + q, d).start()

                which = jnp.where(upper == core, 0, 1)
                x_all[slot_of((k + q) // 2, chip), :] = x_buf[which, rows_of(k + q), :]

    def backward_start(k, span):
        rows = wide_rows(k, span)
        for p in range(PIECES):
            cols = cols_of(p)

            if span == 1:

                @pl.when(stage < last)
                def _():
                    b_copy(k, p).wait_recv()

            s_buf[0, rows, cols] = (
                g_buf[rows, cols].astype(jnp.float32) * slopes[rows, cols].astype(jnp.float32)
            ).astype(jnp.bfloat16)
            for q in range(span):
                s_copy(k + q, p).start()

    def backward_own(k, span):
        @pl.when(stage > 0)
        def _():
            acc[pl.ds(0, span * CHUNK), :] = mm(s_buf[0, wide_rows(k, span), :], w_bwd[0])

    def backward_rest(k, span):
        rows, some = wide_rows(k, span), pl.ds(0, span * CHUNK)
        for p in range(PIECES):
            for q in range(span):
                s_copy(k + q, p).wait_recv()
            cols = cols_of(p)
            if p < PIECES - 1:

                @pl.when(stage > 0)
                def _():
                    acc[some, :] += mm(s_buf[1, rows, cols], w_bwd[1, cols, :])

        @pl.when(stage > 0)
        def _():
            if span == 1:

                @pl.when(stage < last)
                def _():
                    for p in range(PIECES):
                        f_copy(k, p).wait_send()

            for p in range(PIECES):
                cols = cols_of(p)
                back = acc[some, cols] + mm(s_buf[1, rows, end], w_bwd[1, end, cols])
                h_send[rows, cols] = (
                    g_buf[rows, cols].astype(jnp.float32) + back
                ).astype(jnp.bfloat16)
                b_copy(k, p).start()
            for q in range(1, span):
                for p in range(PIECES):
                    b_copy(k + q, p).start()

    def backward_end(k, span):
        for q in range(span):

            @pl.when(lax.rem(k + q, 2) == core)
            def _():
                @pl.when(jnp.logical_not(hold_s) | (k + q < HELD))
                def _():
                    for d in (5, 3, 7, 1):
                        sa_send(k + q, d).start()

                for d in (4, 2, 6):
                    sa_send(k + q, d).start()

                which = jnp.where(lax.rem(ring, 2) == core, 0, 1)
                cols = pl.ds(pl.multiple_of(side * QUAD, QUAD), QUAD)
                s_all[slot_of((k + q) // 2, chip), :] = s_buf[which, rows_of(k + q), cols]

    def forward(k, span):
        forward_own(k, span)
        forward_rest(k, span)
        forward_end(k, span)

    def backward(k, span):
        backward_start(k, span)
        backward_own(k, span)
        backward_rest(k, span)
        backward_end(k, span)

    tile = 256

    def turn():
        loads[2].wait()

        @pl.when(stage > 0)
        def _():
            def step(i, carry):
                at = pl.ds(pl.multiple_of(i * tile, tile), tile)
                for j in range(HALF // tile):
                    to = pl.ds(j * tile, tile)
                    w_bwd[0, to, at] = w_fwd[0, at, to].T
                    w_bwd[1, to, at] = w_raw[at, to].T
                return carry

            lax.fori_loop(0, HALF // tile, step, 0)

        load = pltpu.make_async_copy(inv_in, p_raw.at[0], load_sem.at[0])
        load.start()
        load.wait()
        p_in[...] = p_raw[0].astype(jnp.bfloat16)
        p_out[...] = jnp.zeros_like(p_out)

        def step(i, carry):
            pair = pltpu.make_async_copy(inv_out.at[pl.ds(2 * i, 2)], p_raw, load_sem.at[0])
            pair.start()
            pair.wait()
            p_out[i, 0:BLOCK, 0:BLOCK] = p_raw[0].astype(jnp.bfloat16)
            p_out[i, BLOCK:TWIN, BLOCK:TWIN] = p_raw[1].astype(jnp.bfloat16)
            return carry

        lax.fori_loop(0, NBLK // 2, step, 0)

    gi_copy = remote(gi_send, gi_recv, gi_sem.at[0], gi_sem.at[1], sibling)

    def collect_x():
        def arrive(i, carry):
            for d in (2, 4, 6) + INDIRECT:
                xa_recv(i, d).wait_recv()

            @pl.when(jnp.logical_not(passing))
            def _():
                for d in DIRECT:
                    xa_recv(i, d).wait_recv()

            return carry

        lax.fori_loop(0, SHARE, arrive, 0)

        def turn_x(j, carry):
            cols = pl.ds(pl.multiple_of(j * tile, tile), tile)
            x_turned[cols, :] = x_all[:, cols].T
            return carry

        lax.fori_loop(0, HALF // tile, turn_x, 0)
        at = pl.ds(pl.multiple_of(quarter * TWIN, TWIN), TWIN)
        square[...] = mm(x_turned[at, :], x_all[:, at]) * (1.0 / TOKENS)
        for e in range(2):
            span = slice(e * BLOCK, (e + 1) * BLOCK)

            @pl.when(core == e)
            def _():
                gram_in[...] = square[span, span]

            @pl.when(core != e)
            def _():
                gi_send[...] = square[span, span]

        gi_copy.start()

    ahead = jnp.where(stage == last, 1, jnp.where(stage == last - 1, AHEAD, CHUNKS))

    def s_arrive(i, carry):
        for d in range(1, CHIPS):
            sa_recv(i, d).wait_recv()
        return carry

    def slot(t, carry):
        kf = jnp.where(stage == last, jnp.where(t == 0, 0, CHUNKS - 1), t)
        kb = jnp.where(stage == last, kf, t - (ahead - 1))
        alone = (stage < last) | (t == 0) | (t == CHUNKS // 2)

        @pl.when(alone & (kf < CHUNKS))
        def _():
            forward(kf, 1)

        @pl.when((t == CHUNKS - 1) & hold_x)
        def _():
            def step(i, carry):
                for d in DIRECT:
                    xa_send(2 * i + core, d).start()
                return carry

            lax.fori_loop(0, SHARE, step, 0)

        @pl.when((t == CHUNKS - 1) & passing)
        def _():
            pass_all()

        @pl.when((t == CHUNKS - 1) & (2 * stage + CHUNKS <= 2 * last))
        def _():
            turn()

        @pl.when((t == CHUNKS - 1) & (stage == 0))
        def _():
            collect_x()

        @pl.when((stage == 0) & (kb == CHUNKS - 1))
        def _():
            lax.fori_loop(0, SHARE - 2, s_arrive, 0)

        @pl.when(alone & (kb >= 0))
        def _():
            backward(kb, 1)

        @pl.when(jnp.logical_not(alone))
        def _():
            forward(2 * t - 1, 2)
            backward(2 * t - 1, 2)

        return carry

    @pl.when(2 * stage + CHUNKS > 2 * last)
    def _():
        turn()

    lax.fori_loop(0, jnp.where(stage == last, CHUNKS // 2 + 1, CHUNKS + ahead - 1), slot, 0)

    @pl.when(hold_s)
    def _():
        def step(k, carry):
            @pl.when(lax.rem(k, 2) == core)
            def _():
                for d in range(1, CHIPS, 2):
                    sa_send(k, d).start()

            return carry

        lax.fori_loop(HELD, CHUNKS, step, 0)

    @pl.when(stage > 0)
    def _():
        collect_x()

    lax.fori_loop(jnp.where(stage == 0, SHARE - 2, 0), SHARE, s_arrive, 0)

    def block(j, parity):
        rows = pl.ds(pl.multiple_of((2 * j + parity) * BLOCK, 16), BLOCK)
        return mm(x_turned[rows, :], s_all[...])

    def e_copy(n):
        return remote(e_send.at[n], e_recv.at[n], e_send_sem.at[n], e_recv_sem.at[n], sibling)

    def o_copy(n, j):
        owner = {"dp": (2 * upper + j // 2) * 4 + lax.rem(j, 2) * 2 + core}
        return remote(
            e_send.at[n], o_recv.at[quarter], o_send_sem.at[n], o_recv_sem.at[quarter], owner
        )

    def share(n, carry):
        e_send[n] = block(lax.rem(quarter + 1 + n, 4), 1 - core).astype(jnp.bfloat16)
        e_copy(n).start()
        return carry

    lax.fori_loop(0, 4, share, 0)

    def reduce(n, carry):
        j = lax.rem(quarter + 1 + n, 4)
        ours = block(j, core)
        e_copy(n).wait_recv()
        whole = (ours + e_recv[n].astype(jnp.float32)).astype(jnp.bfloat16)

        @pl.when(n < 3)
        def _():
            e_copy(n).wait_send()
            e_send[n] = whole
            o_copy(n, j).start()

        @pl.when(n == 3)
        def _():
            o_recv[quarter] = whole

        return carry

    lax.fori_loop(0, 4, reduce, 0)

    cols = pl.ds(pl.multiple_of(upper * TWIN, TWIN), TWIN)
    square[...] = gram(s_all[:, cols], s_all[:, cols]) * (1.0 / TOKENS)

    def go_remote(e, device):
        return remote(go_send.at[e], go_recv.at[core], go_send_sem.at[e], go_recv_sem.at[core], device)

    for e in range(2):
        span = slice(e * BLOCK, (e + 1) * BLOCK)
        go_send[e] = square[span, span]

        @pl.when(go_rank(e) == rank)
        def _():
            pltpu.make_async_copy(go_send.at[e], go_recv.at[core], go_recv_sem.at[core]).start()

        @pl.when(go_rank(e) != rank)
        def _():
            go_remote(e, {"dp": go_rank(e)}).start()

    def condition(n, carry):
        who = lax.rem(quarter + 4 - n, 4)

        @pl.when(n > 0)
        def _():
            here = o_recv.at[who]
            remote(here, here, o_send_sem.at[0], o_recv_sem.at[who], sibling).wait_recv()

        left = mm(p_in[...], o_recv[who]).astype(jnp.bfloat16)
        for j in range(2):
            right = mm(left[:, j * TWIN : (j + 1) * TWIN], p_out[2 * who + j])
            at = pl.ds(pl.multiple_of(who * QUAD + j * TWIN, TWIN), TWIN)
            update[:, at] = (right * (1.0 / TOKENS**0.5)).astype(jnp.bfloat16)
        return carry

    lax.fori_loop(0, 1, condition, 0)

    def drain(k, carry):
        for p in range(PIECES):

            @pl.when((stage < last) & (stage == 0))
            def _():
                f_copy(k, p).wait_send()

            @pl.when(stage > 0)
            def _():
                x_copy(k, p).wait_send()
                b_copy(k, p).wait_send()

            s_copy(k, p).wait_send()

        @pl.when((stage == 0) & (k // SHARE == core))
        def _():
            for h in range(2):
                i_copy(k, h).wait_send()

        @pl.when(lax.rem(k, 2) == core)
        def _():
            for d in range(1, CHIPS):
                sa_send(k, d).wait_send()
            for d in (2, 4, 6) + DIRECT:
                xa_send(k, d).wait_send()

            @pl.when(passing)
            def _():
                for d in DIRECT:
                    pass_on(k // 2, d).wait_send()

            @pl.when(jnp.logical_not(passing))
            def _():
                for d in INDIRECT:
                    xa_send(k, d).wait_send()


        return carry

    lax.fori_loop(0, CHUNKS, drain, 0)
    gi_copy.wait()
    gram_in[...] += gi_recv[...]
    for e in range(2):
        own = go_source(e) == rank

        @pl.when(own)
        def _():
            pltpu.make_async_copy(go_send.at[0], go_recv.at[e], go_recv_sem.at[e]).wait()

        @pl.when(jnp.logical_not(own))
        def _():
            here = go_recv.at[e]
            remote(here, here, go_send_sem.at[0], go_recv_sem.at[e], sibling).wait_recv()

    gram_out[...] = go_recv[0] + go_recv[1]

    lax.fori_loop(1, 4, condition, 0)

    e_copy(3).wait_send()
    for n in range(3):
        o_copy(n, lax.rem(quarter + 1 + n, 4)).wait_send()
    for e in range(2):

        @pl.when(go_rank(e) != rank)
        def _():
            go_remote(e, sibling).wait_send()


def run_pipeline(counts, tokens, cotangent, matrix, inverse_in, inverse_out):
    dma = pltpu.SemaphoreType.DMA
    any_space = pl.BlockSpec(memory_space=pl.ANY)
    in_vmem = pl.BlockSpec(memory_space=pltpu.VMEM)
    pieces = (CHUNKS, PIECES)
    peers = (SHARE, CHIPS - 1)
    bf16, f32 = jnp.bfloat16, jnp.float32
    return pl.pallas_call(
        functools.partial(pipeline, lax.axis_size("section")),
        out_shape=[
            jax.ShapeDtypeStruct((BLOCK, D), bf16),
            jax.ShapeDtypeStruct((BLOCK, BLOCK), f32),
            jax.ShapeDtypeStruct((BLOCK, BLOCK), f32),
        ],
        in_specs=[pl.BlockSpec(memory_space=pltpu.SMEM)] + [any_space] * 5,
        out_specs=[in_vmem] * 3,
        scratch_shapes=[
            pltpu.VMEM((2, PAIR, HALF), bf16),
            pltpu.VMEM((2, PAIR, HALF), bf16),
            pltpu.VMEM((PAIR, HALF), bf16),
            pltpu.VMEM((PAIR, HALF), bf16),
            pltpu.VMEM((PAIR, HALF), bf16),
            pltpu.VMEM((2, HALF, HALF), bf16),
            pltpu.VMEM((2, HALF, HALF), bf16),
            pltpu.VMEM((HALF, HALF), bf16),
            pltpu.VMEM((2 * CHUNK, HALF), f32),
            pltpu.VMEM((SEEN, HALF), bf16),
            pltpu.VMEM((HALF, SEEN), bf16),
            pltpu.VMEM((SEEN, QUAD), bf16),
            pltpu.VMEM((4, BLOCK, QUAD), bf16),
            pltpu.VMEM((4, BLOCK, QUAD), bf16),
            pltpu.VMEM((4, BLOCK, QUAD), bf16),
            pltpu.VMEM((2, BLOCK, BLOCK), f32),
            pltpu.VMEM((BLOCK, BLOCK), bf16),
            pltpu.VMEM((NBLK // 2, TWIN, TWIN), bf16),
            pltpu.VMEM((TWIN, TWIN), f32),
            pltpu.VMEM((BLOCK, BLOCK), f32),
            pltpu.VMEM((BLOCK, BLOCK), f32),
            pltpu.VMEM((2, BLOCK, BLOCK), f32),
            pltpu.VMEM((2, BLOCK, BLOCK), f32),
            dma((5,)),
            dma((1,)),
            dma((1,)),
        ]
        + [dma(pieces)] * 8
        + [dma(peers)] * 2
        + [dma((SHARE, 2))]
        + [dma(peers)] * 2
        + [dma((4,))] * 4
        + [dma((2,))] * 3,
        compiler_params=pltpu.CompilerParams(
            collective_id=0, has_side_effects=True, vmem_limit_bytes=62 * 2**20
        ),
        name="pipeline",
    )(counts, tokens, cotangent, matrix, inverse_in, inverse_out)


def hand_over(*refs):
    for i in range(3):
        refs[3 + i][...] = refs[i][...]


def outputs(*arrays):
    in_vmem = pl.BlockSpec(memory_space=pltpu.VMEM)
    return pl.pallas_call(
        hand_over,
        out_shape=[jax.ShapeDtypeStruct(a.shape, a.dtype) for a in arrays],
        in_specs=[in_vmem] * 3,
        out_specs=[in_vmem] * 3,
        name="outputs",
    )(*arrays)


def shards(tokens, cotangent, live_counts, weight, inverse_in, inverse_out):
    results = run_pipeline(
        live_counts[0], tokens, cotangent, weight[0], inverse_in[0, 0], inverse_out[0]
    )
    update, owned_in, owned_out = outputs(*results)
    return (update[None], owned_in[None, None], owned_out[None, None])


def solution(mesh):
    in_specs = (
        P("dp", None),
        P("dp", None),
        P("dp", None),
        P("section", None, None),
        P("section", "dp", None, None),
        P("section", None, None, None),
    )
    out_specs = (
        P("section", "dp", None),
        P("section", "dp", None, None),
        P("section", "dp", None, None),
    )
    return jax.shard_map(shards, mesh=mesh, in_specs=in_specs, out_specs=out_specs, check_vma=False)
```
